32 devices in a mesh: mer: 8 (over z, y), az: 4 (over x, core).
Axes of the slice: x: 2, y: 2, z: 4, core: 2. Of those that a mesh axis runs over, the one named last changes fastest.
Arguments:
- displacement: float32 [3, 5, 64, 512], P(None, None, 'mer', 'az'), may hold values from -6 to 6
- velocity: float32 [3, 5, 64, 512], P(None, None, 'mer', 'az'), may hold values from -1.5 to 1.5
- modulus: float32 [1, 16], P(None, 'mer'), may hold values from 0.5 to 2
- hoop_strength: float32 [1, 16], P(None, 'mer'), may hold values from 0.5 to 2
- coupling: float32 [1, 16], P(None, 'mer'), may hold values from -1 to 1
- density: float32 [1, 16], P(None, 'mer'), may hold values from 0.5 to 2
- order_count: int32 [1, 16], P(None, 'mer'), may hold values from 1 to 256
- point_element: int32 [512, 2], P('mer'), may hold values from 0 to 15, as said below
- point_local: float32 [512, 2], P('mer'), may hold values from -1 to 1
- azimuth_scale: float32 [512], P('mer'), may hold values from 0.5 to 2
- point_owner: int32 [512, 1], P('mer'), may hold values from 0 to 7; in each aligned block of 64 rows (0 to 63, 64 to 127, ...) at most 16 rows name the same one
- point_cell: int32 [512], P('mer'), may hold values from 0 to 31
- adjoint_strain: float32 [9, 8, 32, 512], P(None, None, 'mer', 'az'), may hold values from -6 to 6
Outputs:
- final_displacement: float32 [3, 5, 64, 512], P(None, None, 'mer', 'az')
- kernel: float32 [8, 32, 512], P(None, 'mer', 'az')
The draws below stay inside these ranges and needn't reach their ends.
Inputs may be any that keep to these rules, and one draw needn't show every extreme that they name: `point_element`: points p with p // 64 = i lie in colatitude elements i * 2 to (i + 1) * 2 - 1; the first column is below 1. `point_owner`: among the points of one device (aligned blocks of 64 points) no owner is named more than 16 times, a bound that some block reaches.
All inputs are finite; a program needn't handle non-finite values.
Results may differ from the reference program's by a relative error of at most 0.0003.
Values sent between devices are 32-bit elements; how exact they have to be, the bound alone decides.
A program may use at most 64 MiB of HBM per device.

```python
import math
import jax
import jax.numpy as jnp
import numpy as np
from jax import lax

ER = 1
EC_DEV = 2
POINTS_DEV = 64
ORDERS = 256
STEPS = 3
VDEPTH = 8
VLAT_DEV = 4
EC = 16
NR = 5
NC = 64
COEFS = 512
NPHI = 512
POINTS = 512
CAP = 16
VLAT = 32
N_MER = 8
N_AZ = 4


def draw_point_element(key, part):
    key_rows, key_cols = jax.random.split(jax.random.fold_in(key, 17))
    row_draw = jax.random.randint(key_rows, (POINTS,), 0, ER, dtype=jnp.int32)
    device_of = jnp.arange(POINTS, dtype=jnp.int32) // POINTS_DEV
    col_draw = device_of * EC_DEV + jax.random.randint(key_cols, (POINTS,), 0, EC_DEV, dtype=jnp.int32)
    return jnp.stack([row_draw, col_draw], axis=1).astype(jnp.int32)


def plant(values, stream_key, least, high):
    longest = values.shape.index(max(values.shape))
    spots = []
    for shift in (0, 1):
        where = [jax.random.randint(jax.random.fold_in(stream_key, axis), (), 0, length) for axis, length in enumerate(values.shape)]
        where[longest] = (where[longest] + shift) % values.shape[longest]
        spots.append(tuple(where))
    return values.at[spots[0]].set(least).at[spots[1]].set(high)


def shard_levels(rng, dims, cuts, low, high):
    level, own = 1.0, jax.random.fold_in(rng, 6)
    for dim, shards_of in cuts:
        steps = jnp.exp(jax.random.uniform(jax.random.fold_in(own, dim), (shards_of,), jnp.float32, low / len(cuts), high / len(cuts)))
        level = level * jnp.repeat(steps, dims[dim] // shards_of).reshape([-1 if axis == dim else 1 for axis in range(len(dims))])
    return level


def assign_block(stream_key, own, number, rows, number_of, top, limit, skew):
    order = jax.random.permutation(stream_key, number_of)
    packed, usual = portions_of(number_of, rows * top, limit, skew, True), portions_of(number_of, rows * top, limit, skew, False)
    places = jnp.arange(number_of)

    def named(lengths, rotation):
        used = int((lengths > 0).sum())
        fixed = max(1, used // 4)
        shifted = fixed + (places - fixed + rotation * (used - fixed)) % max(1, number_of - fixed)
        return jnp.zeros((number_of,), jnp.int32).at[order[jnp.where(places < fixed, places, shifted)]].set(jnp.asarray(lengths, jnp.int32))

    lengths = jnp.where(number % 4 == 0, named(packed, number // 4), named(usual, number - number // 4 - 1))
    mixed = jax.random.permutation(jax.random.fold_in(own, 3), number_of)
    giver, taker = mixed[0:number_of // 2 * 2:2], mixed[1:number_of // 2 * 2:2]
    room = jnp.minimum(lengths[giver] - 1, limit - lengths[taker]) // 2
    room = jnp.where((giver == order[0]) | (taker == order[0]) | (lengths[taker] == 0), 0, jnp.maximum(room, 0))
    shifted = jax.random.randint(jax.random.fold_in(own, 4), (number_of // 2,), 0, 1 << 20) % (room + 1)
    lengths = lengths.at[giver].add(-shifted).at[taker].add(shifted)
    labels = jnp.searchsorted(jnp.cumsum(lengths), jnp.arange(rows * top), side="right").astype(jnp.int32)
    grid = labels.reshape(top, rows).T
    grid = grid[jax.random.permutation(jax.random.fold_in(own, 1), rows)]
    rotation = jax.random.randint(jax.random.fold_in(own, 2), (rows, 1), 0, top)
    return jnp.take_along_axis(grid, (jnp.arange(top)[None, :] + rotation) % top, axis=1)


def portions_of(amount, total, reach, slope, full):
    weights = [(1 << 20) // math.isqrt(rank ** slope) + 1 for rank in range(1, amount + 1)]
    largest = reach if full else min(reach, max(-(-total // amount), total * weights[0] // sum(weights)))
    least = 1 if total - largest >= amount - 1 else 0
    counts, rest = [largest] + [least] * (amount - 1), total - largest - least * (amount - 1)
    while rest > 0:
        movable = [i for i in range(1, amount) if counts[i] < largest] or [i for i in range(1, amount) if counts[i] < reach]
        mass, remaining = sum([weights[i] for i in movable]), rest
        for i in movable:
            extra = min(reach - counts[i], max(1, remaining * weights[i] // mass), rest)
            counts[i] = counts[i] + extra
            rest = rest - extra
    return np.array(counts)


def gaussian(key, dims, width, limit, cuts=(), kind=jnp.bfloat16):
    entries = width * jax.random.normal(key, dims, jnp.float32)
    if cuts:
        entries = entries * shard_levels(key, dims, cuts, -0.22, 0.18)
    return jnp.clip(entries, -limit, limit).astype(kind)


def setup_inputs(seed: int = 0) -> dict:
    key_list = jax.random.split(jax.random.key(seed), 14)
    displacement = gaussian(key_list[0], (3, NR, NC, COEFS), 1.0, 6.0, ((2, 8), (3, 4)), jnp.float32)
    velocity = gaussian(key_list[1], (3, NR, NC, COEFS), 0.25, 1.5, ((2, 8), (3, 4)), jnp.float32)
    modulus = jnp.clip(jnp.exp(math.log(2.0) - 1.3862944 * jax.random.uniform(key_list[2], (ER, EC), jnp.float32) ** shard_levels(key_list[2], (ER, EC), ((1, 8),), -0.2, 0.2)), 0.5, 2.0)
    hoop_strength = jnp.clip(jnp.exp(math.log(2.0) - 1.3862944 * jax.random.uniform(key_list[3], (ER, EC), jnp.float32) ** shard_levels(key_list[3], (ER, EC), ((1, 8),), -0.2, 0.2)), 0.5, 2.0)
    coupling = jnp.clip(jax.random.uniform(key_list[4], (ER, EC), jnp.float32, -1.0, 1.0) * shard_levels(key_list[4], (ER, EC), ((1, 8),), -0.4, 0.0), -1.0, 1.0)
    density = jnp.clip(jnp.exp(math.log(2.0) - 1.3862944 * jax.random.uniform(key_list[5], (ER, EC), jnp.float32) ** shard_levels(key_list[5], (ER, EC), ((1, 8),), -0.2, 0.2)), 0.5, 2.0)
    order_count = plant(jax.random.randint(key_list[6], (ER, EC), 1, ORDERS + 1), jax.random.fold_in(key_list[6], 1), 1, ORDERS).astype(jnp.int32)
    point_element = draw_point_element(jax.random.fold_in(key_list[13], 71), 0)
    point_local = jnp.clip(jax.random.uniform(key_list[8], (POINTS, 2), jnp.float32, -1.0, 1.0) * shard_levels(key_list[8], (POINTS, 2), ((0, 8),), -0.4, 0.0), -1.0, 1.0)
    azimuth_scale = jnp.clip(jnp.exp(math.log(2.0) - 1.3862944 * jax.random.uniform(key_list[9], (POINTS,), jnp.float32) ** shard_levels(key_list[9], (POINTS,), ((0, 8),), -0.2, 0.2)), 0.5, 2.0)
    point_owner_keys = jax.random.split(jax.random.fold_in(key_list[10], 1), POINTS // POINTS_DEV)
    point_owner_turns = jax.random.permutation(jax.random.fold_in(key_list[10], 3), POINTS // POINTS_DEV)
    point_owner = jax.vmap(lambda own, number: assign_block(jax.random.fold_in(key_list[10], 2), own, number, POINTS_DEV, N_MER, 1, CAP, 2))(point_owner_keys, point_owner_turns).reshape((POINTS, 1))
    point_cell = plant(jax.random.randint(key_list[11], (POINTS,), 0, VDEPTH * VLAT_DEV), jax.random.fold_in(key_list[11], 1), 0, (VDEPTH * VLAT_DEV) - 1).astype(jnp.int32)
    adjoint_strain = gaussian(key_list[12], (9, VDEPTH, VLAT, NPHI), 1.0, 6.0, ((2, 8), (3, 4)), jnp.float32)
    return dict(displacement=displacement, velocity=velocity, modulus=modulus, hoop_strength=hoop_strength, coupling=coupling, density=density, order_count=order_count, point_element=point_element, point_local=point_local, azimuth_scale=azimuth_scale, point_owner=point_owner, point_cell=point_cell, adjoint_strain=adjoint_strain)


step_scale = 0.015
smooth_rate = 0.125

def gll_tables():
    gll_nodes = np.array([-1.0, -math.sqrt(3.0 / 7.0), 0.0, math.sqrt(3.0 / 7.0), 1.0])
    gll_weights = np.array([0.1, 49.0 / 90.0, 32.0 / 45.0, 49.0 / 90.0, 0.1])
    derivative = np.zeros((5, 5))
    for i in range(5):
        for j in range(5):
            if i == j:
                derivative[i, j] = sum((1.0 / (gll_nodes[i] - gll_nodes[l]) for l in range(5) if l != i))
            else:
                scale_i = np.prod([gll_nodes[i] - gll_nodes[l] for l in range(5) if l != i])
                scale_j = np.prod([gll_nodes[j] - gll_nodes[l] for l in range(5) if l != j])
                derivative[i, j] = scale_i / (scale_j * (gll_nodes[i] - gll_nodes[j]))
    return (gll_nodes, gll_weights, derivative)

def lagrange(position):
    gll_nodes = gll_tables()[0]
    basis_values = []
    basis_slopes = []
    for j in range(5):
        others = [l for l in range(5) if l != j]
        product = jnp.ones_like(position)
        for l in others:
            product = product * (position - float(gll_nodes[l])) / float(gll_nodes[j] - gll_nodes[l])
        gradient_sum = jnp.zeros_like(position)
        for l in others:
            summand = jnp.ones_like(position) / float(gll_nodes[j] - gll_nodes[l])
            for i in others:
                if i != l:
                    summand = summand * (position - float(gll_nodes[i])) / float(gll_nodes[j] - gll_nodes[i])
            gradient_sum = gradient_sum + summand
        basis_values.append(product)
        basis_slopes.append(gradient_sum)
    return (jnp.stack(basis_values, axis=1), jnp.stack(basis_slopes, axis=1))

def to_elements(nodal):
    count_rows = (nodal.shape[1] - 1) // 4
    count_cols = (nodal.shape[2] - 1) // 4
    radial = jnp.stack([nodal[:, a:a + 4 * count_rows:4] for a in range(5)], axis=2)
    return jnp.stack([radial[:, :, :, b:b + 4 * count_cols:4] for b in range(5)], axis=4)

def from_elements(element_values):
    components, count_rows, _, count_cols, _, coef_width = element_values.shape
    radial = jnp.zeros((components, 4 * count_rows + 1, count_cols, 5, coef_width), element_values.dtype)
    for a in range(5):
        radial = radial.at[:, a:a + 4 * count_rows:4].add(element_values[:, :, a])
    assembled = jnp.zeros((components, 4 * count_rows + 1, 4 * count_cols + 1, coef_width), element_values.dtype)
    for b in range(5):
        assembled = assembled.at[:, :, b:b + 4 * count_cols:4].add(radial[:, :, :, b])
    return assembled

def quadrature_table():
    gll_weights = jnp.asarray(gll_tables()[1], jnp.float32)
    return gll_weights[:, None] * gll_weights[None, :]

def rotate(vector, order_ratio):
    lane_index = lax.broadcasted_iota(jnp.int32, vector.shape, vector.ndim - 1)
    is_even = lane_index % 2 == 0
    return jnp.where(is_even, jnp.roll(vector, -1, axis=-1), -jnp.roll(vector, 1, axis=-1)) * order_ratio

def element_mass(density):
    quadrature = quadrature_table()
    return (density[:, None, :, None] * quadrature[None, :, None, :])[None, :, :, :, :, None]

def element_forces(element_values, modulus, hoop_strength, coupling, order_count, order_index, order_ratio):
    quadrature = quadrature_table()
    derivative = jnp.asarray(gll_tables()[2], jnp.float32)
    highest = lax.Precision.HIGHEST

    def spread(per_element):
        return (per_element[:, None, :, None] * quadrature[None, :, None, :])[:, :, :, :, None]
    stiff_node = spread(modulus)[None]
    hoop_node = spread(hoop_strength)[None]
    couple_node = spread(coupling)
    grad_radial = jnp.einsum('pa,cEaFbk->cEpFbk', derivative, element_values, precision=highest)
    grad_colat = jnp.einsum('qb,cEaFbk->cEaFqk', derivative, element_values, precision=highest)
    back_radial = jnp.einsum('pa,cEpFbk->cEaFbk', derivative, stiff_node * grad_radial, precision=highest)
    back_colat = jnp.einsum('qb,cEaFqk->cEaFbk', derivative, stiff_node * grad_colat, precision=highest)
    forces = -(back_radial + back_colat + hoop_node * (order_ratio * order_ratio) * element_values)
    forces = jnp.stack([forces[0] + couple_node * rotate(element_values[2], order_ratio), forces[1], forces[2] - couple_node * rotate(element_values[0], order_ratio)], axis=0)
    order_mask = order_index[None, None, None, None, :] < order_count[:, None, :, None, None]
    return jnp.where(order_mask[None], forces, 0.0)

def point_gradients(gathered, xi_values, xi_slopes, eta_values, eta_slopes, azimuth_scale, order_ratio):
    highest = lax.Precision.HIGHEST
    nodal_value = jnp.einsum('pa,pb,cpabk->pck', xi_values, eta_values, gathered, precision=highest)
    along_radius = jnp.einsum('pa,pb,cpabk->pck', xi_slopes, eta_values, gathered, precision=highest)
    along_colat = jnp.einsum('pa,pb,cpabk->pck', xi_values, eta_slopes, gathered, precision=highest)
    around_axis = azimuth_scale[:, None, None] * rotate(nodal_value, order_ratio)
    stacked = jnp.stack([along_radius, along_colat, around_axis], axis=2)
    return stacked.reshape(gathered.shape[1], 9, gathered.shape[4])

def fourier_basis(coef_start, coef_count, phi_start, phi_count, total_phi):
    coef_rows = coef_start + lax.broadcasted_iota(jnp.int32, (coef_count, phi_count), 0)
    phi_cols = phi_start + lax.broadcasted_iota(jnp.int32, (coef_count, phi_count), 1)
    wrapped = coef_rows // 2 * phi_cols % total_phi
    angles = wrapped.astype(jnp.float32) * (2.0 * math.pi / total_phi)
    return jnp.where(coef_rows % 2 == 0, jnp.cos(angles), jnp.sin(angles))

def reference(displacement, velocity, modulus, hoop_strength, coupling, density, order_count, point_element, point_local, azimuth_scale, point_owner, point_cell, adjoint_strain):
    highest = lax.Precision.HIGHEST
    block_width = COEFS // N_AZ
    block_total = COEFS // block_width
    nodal_mass = from_elements(element_mass(density))[0, :, :NC]
    xi_values, xi_slopes = lagrange(point_local[:, 0])
    eta_values, eta_slopes = lagrange(point_local[:, 1])
    offsets = jnp.arange(5, dtype=jnp.int32)[None, :]
    row_index = 4 * point_element[:, 0:1] + offsets
    col_index = 4 * point_element[:, 1:2] + offsets

    def one_block(block_number):
        first_coef = block_number * block_width
        current = lax.dynamic_slice_in_dim(displacement, first_coef, block_width, 3)
        previous = current - lax.dynamic_slice_in_dim(velocity, first_coef, block_width, 3)
        order_index = (first_coef + jnp.arange(block_width, dtype=jnp.int32)) // 2
        order_ratio = order_index.astype(jnp.float32) / ORDERS
        closing = jnp.zeros((3, NR, 1, block_width), jnp.float32)
        for step_index in range(STEPS):
            padded = jnp.concatenate([current, closing], axis=2)
            forces = from_elements(element_forces(to_elements(padded), modulus, hoop_strength, coupling, order_count, order_index, order_ratio))[:, :, :NC]
            following = 2.0 * current - previous + step_scale * forces / nodal_mass
            previous, current = (current, following)
        padded = jnp.concatenate([current, closing], axis=2)
        gathered = padded[:, row_index[:, :, None], col_index[:, None, :], :]
        gradients = point_gradients(gathered, xi_values, xi_slopes, eta_values, eta_slopes, azimuth_scale, order_ratio)
        return (current, gradients)
    finals, gradients = lax.map(one_block, jnp.arange(block_total, dtype=jnp.int32))
    final_displacement = jnp.moveaxis(finals, 0, 3).reshape(3, NR, NC, COEFS)
    gradients = jnp.moveaxis(gradients, 0, 2).reshape(POINTS, 9, COEFS)
    basis = fourier_basis(0, COEFS, 0, NPHI, NPHI)
    samples = jnp.einsum('pgk,kj->pgj', gradients, basis, precision=highest) * (1.0 / math.sqrt(ORDERS))
    depth = point_cell // VLAT_DEV
    latitude = point_owner[:, 0] * VLAT_DEV + point_cell % VLAT_DEV
    adjoint_points = adjoint_strain[:, depth, latitude, :]
    contribution = lax.optimization_barrier(jnp.sum(samples * jnp.moveaxis(adjoint_points, 0, 1), axis=1))
    flat_voxel = depth * VLAT + latitude
    raw = jax.ops.segment_sum(contribution, flat_voxel, num_segments=VDEPTH * VLAT).reshape(VDEPTH, VLAT, NPHI)
    framed = jnp.pad(raw, ((1, 1), (1, 1), (0, 0)))
    neighbours = framed[2:, 1:-1] + framed[:-2, 1:-1] + framed[1:-1, 2:] + framed[1:-1, :-2]
    neighbours = neighbours + jnp.roll(raw, 1, axis=2) + jnp.roll(raw, -1, axis=2)
    kernel = raw + smooth_rate * (neighbours - 6.0 * raw)
    return (final_displacement, kernel)
```

```python
import functools
import math

import jax
import jax.numpy as jnp
import ml_dtypes
import numpy as np
from jax import lax
from jax.experimental import pallas as pl
from jax.experimental.pallas import tpu as pltpu
from jax.sharding import PartitionSpec as P

ORDERS = 256
STEPS = 3
step_scale = 0.015
smooth_rate = 0.125
MESH = pl.DeviceIdType.MESH


def gll_tables():
    nodes = np.array([-1.0, -math.sqrt(3.0 / 7.0), 0.0, math.sqrt(3.0 / 7.0), 1.0])
    weights = np.array([0.1, 49.0 / 90.0, 32.0 / 45.0, 49.0 / 90.0, 0.1])
    monomials = np.zeros((5, 5))
    for j in range(5):
        poly = np.array([1.0])
        for l in range(5):
            if l != j:
                poly = np.convolve(poly, np.array([1.0, -nodes[l]]) / (nodes[j] - nodes[l]))
        monomials[j] = poly[::-1]
    slopes = monomials[:, 1:] * np.arange(1, 5)
    derivative = np.array(
        [[sum(slopes[j, p] * nodes[i] ** p for p in range(4)) for j in range(5)] for i in range(5)]
    )
    stiffness = derivative.T @ np.diag(weights) @ derivative
    return weights, monomials, slopes, stiffness


def lane_table(elements, cols, lanes):
    _, monomials, slopes, _ = gll_tables()
    table = np.zeros((9 * (1 + elements), lanes), np.float32)
    for lane in range(lanes):
        half, spot = divmod(lane, lanes // 2)
        a, col = divmod(spot, cols)
        if a > 4 or (half and col):
            continue
        col = cols if half else col
        table[0:5, lane], table[5:9, lane] = monomials[a], slopes[a]
        for e in range(elements):
            b = col - 4 * e
            if 0 <= b <= 4:
                at = 9 * (1 + e)
                table[at : at + 5, lane], table[at + 5 : at + 9, lane] = monomials[b], slopes[b]
    return table


def column_table(elements, cols, lanes):
    weights, _, _, stiffness = gll_tables()
    table = np.zeros((elements, cols + 2, cols, lanes), np.float32)
    for e in range(elements):
        for c in range(cols):
            b = c - 4 * e
            if not 0 <= b <= 4:
                continue
            table[e, 0, c] = weights[b]
            for d in range(cols):
                other = (c - d) % cols - 4 * e
                if 0 <= other <= 4:
                    table[e, 1 + d, c] = stiffness[b, other]
            if cols - 4 * e == 4:
                table[e, cols + 1, c] = stiffness[b, 4]
    return table


def rim_table(cols, lanes):
    _, _, _, stiffness = gll_tables()
    table = np.zeros((cols, cols, lanes), np.float32)
    for d in range(cols):
        for a in range(5):
            other = (a - d) % cols
            if other <= 4:
                table[d, a] = stiffness[a, other]
    return table


def basis_tables(az_count, width, phi_width):
    coefs, phis = az_count * width, az_count * phi_width
    k, j = np.arange(coefs)[:, None], np.arange(phis)[None, :]
    angles = (k // 2) * j % (2 * ORDERS) * (2.0 * math.pi / (2 * ORDERS))
    basis = np.where(k % 2 == 0, np.cos(angles), np.sin(angles)) / math.sqrt(ORDERS)
    basis = basis.reshape(az_count, width, az_count, phi_width).transpose(0, 2, 1, 3)
    basis = basis.astype(np.float32)
    high = basis.astype(ml_dtypes.bfloat16)
    low = (basis - high.astype(np.float32)).astype(ml_dtypes.bfloat16)
    return high, low


def halves(x):
    high = x.astype(jnp.bfloat16)
    return high, (x - high.astype(jnp.float32)).astype(jnp.bfloat16)


def dot(x, y):
    return jnp.dot(x, y, preferred_element_type=jnp.float32)


def dot3(x, y):
    (xh, xl), (yh, yl) = x, y
    return dot(xh, yh) + (dot(xl, yh) + dot(xh, yl))


def kernel(
    n, az, disp, vel, modulus, hoop, coupling, density, orders, element, local, scale, owner, cell,
    adjoint, bhi, blo, lanes_t, cols_t, rim_t, out_u, out_k,
    halo_out, halo_in, dens_out, dens_in, fl_out, fr_out, fl_in, fr_in, meta, gathered, mix,
    adj_all, bh, bl, part_out, part_in, face_out, face_in,
    halo_s, halo_r, dens_s, dens_r, f_s, f_r, meta_s, meta_r, adj_s, adj_r, ga_s, ga_r, gb_s, gb_r,
    part_s, part_r, face_s, face_r, b_s,
):
    o, q = lax.axis_index("mer"), lax.axis_index("az")
    comps, nr, cols, width = disp.shape
    elements = modulus.shape[1]
    points = owner.shape[0]
    slot = gathered.shape[2]
    nodes = nr * cols
    cells = adjoint.shape[1]
    depth = face_in.shape[2]
    weights, _, _, stiffness = gll_tables()
    has_left, has_right = o > 0, o < n - 1

    halo_in[...] = jnp.zeros_like(halo_in)
    dens_in[...] = jnp.zeros_like(dens_in)
    fl_in[...] = jnp.zeros_like(fl_in)
    fr_in[...] = jnp.zeros_like(fr_in)
    face_in[...] = jnp.zeros_like(face_in)
    gathered[:, :, nodes:, :] = jnp.zeros((n, comps, slot - nodes, width), jnp.float32)

    barrier = pltpu.get_barrier_semaphore()

    @pl.loop(1, n)
    def _(h):
        pl.semaphore_signal(barrier, inc=1, device_id=(lax.rem(o + h, n), q), device_id_type=MESH)

    for h in range(1, az):
        r = lax.rem(q + h, az)
        pl.semaphore_signal(barrier, inc=1, device_id=(o, r), device_id_type=MESH)

        @pl.when(has_left)
        def _():
            pl.semaphore_signal(barrier, inc=1, device_id=(o - 1, r), device_id_type=MESH)

        @pl.when(has_right)
        def _():
            pl.semaphore_signal(barrier, inc=1, device_id=(o + 1, r), device_id_type=MESH)

    basis_copies = [
        pltpu.make_async_copy(bhi.at[q], bh, b_s.at[0]),
        pltpu.make_async_copy(blo.at[q], bl, b_s.at[1]),
    ]
    for copy in basis_copies:
        copy.start()

    row = lax.broadcasted_iota(jnp.int32, (cols, width), 0)
    lane = lax.broadcasted_iota(jnp.int32, (1, width), 1)
    u = [disp[:, a] for a in range(nr)]
    v = [vel[:, a] for a in range(nr)]

    def first_column(values):
        total = jnp.zeros((comps, cols, width), jnp.float32)
        for a in range(nr):
            total = jnp.where((row == a)[None], values[a][:, 0:1, :], total)
        return total

    halo_out[0:comps] = first_column(u)
    halo_out[comps : 2 * comps] = first_column(v)
    halo_out[2 * comps] = jnp.full((cols, width), density[0, 0])
    dens_out[...] = jnp.full((cols, width), density[0, elements - 1])
    eye = lax.broadcasted_iota(jnp.int32, (points, width), 0) == lax.broadcasted_iota(
        jnp.int32, (points, width), 1
    )

    def as_row(column):
        return jnp.sum(jnp.where(eye, column, 0.0), axis=0, keepdims=True)

    def as_column(line):
        return jnp.sum(jnp.where(eye, line, 0.0), axis=1, keepdims=True)

    spare = jnp.zeros((1, width - points), jnp.float32) if width > points else None

    def wide(line):
        return line if spare is None else jnp.concatenate([line, spare], axis=1)

    meta[o] = jnp.concatenate(
        [
            as_row(local[:, 0:1]),
            as_row(local[:, 1:2]),
            as_row((element[:, 1:2] % elements).astype(jnp.float32)),
            as_row(owner[:, 0:1].astype(jnp.float32)),
            wide(scale[...]),
            wide(cell[...].astype(jnp.float32)),
            jnp.zeros((2, width), jnp.float32),
        ],
        axis=0,
    )

    pl.semaphore_wait(
        barrier,
        n - 1 + (az - 1) * (1 + has_left.astype(jnp.int32) + has_right.astype(jnp.int32)),
    )

    def remote(src, dst, send, recv, device):
        return pltpu.make_async_remote_copy(
            src_ref=src, dst_ref=dst, send_sem=send, recv_sem=recv,
            device_id=device, device_id_type=MESH,
        )

    to_left = lambda: remote(halo_out, halo_in, halo_s, halo_r, (o - 1, q))
    to_right = lambda: remote(dens_out, dens_in, dens_s, dens_r, (o + 1, q))
    pl.when(has_left)(lambda: to_left().start())
    pl.when(has_right)(lambda: to_right().start())

    def meta_copy(h):
        return remote(meta.at[o], meta.at[o], meta_s.at[h], meta_r.at[h], (lax.rem(o + h, n), q))

    pl.loop(1, n)(lambda h: meta_copy(h).start())

    def adj_copy(h):
        return remote(
            adjoint, adj_all.at[h], adj_s.at[h], adj_r.at[h], (o, lax.rem(q + az - h, az))
        )

    for h in range(1, az):
        adj_copy(h).start()

    order = (q * width + lane) // 2
    ratio = order.astype(jnp.float32) / ORDERS
    even = (lane % 2 == 0)
    keep = [jnp.where(order < orders[0, e], 1.0, 0.0) for e in range(elements)]
    mod = [modulus[0, e] * keep[e] for e in range(elements)]
    hp = [hoop[0, e] * keep[e] * (ratio * ratio) for e in range(elements)]
    cp = [coupling[0, e] * keep[e] * ratio for e in range(elements)]
    last = elements - 1
    w_end = float(weights[4])

    def blend(per_element, which):
        total = per_element[0] * cols_t[0, which]
        for e in range(1, elements):
            total = total + per_element[e] * cols_t[e, which]
        return total

    c_radial, c_hoop, c_pair = blend(mod, 0), blend(hp, 0), blend(cp, 0)
    c_colat = [blend(mod, 1 + d) for d in range(cols)]
    c_rim = mod[last] * cols_t[last, cols + 1]
    w_rim = jnp.zeros((cols, width), jnp.float32)
    for a in range(nr):
        w_rim = jnp.where(row == a, float(weights[a]), w_rim)
    r_radial = [mod[last] * w_end * rim_t[d] for d in range(cols)]
    r_radial[0] = r_radial[0] + w_rim * (
        mod[last] * float(stiffness[4, 4]) + hp[last] * w_end
    )
    r_pair = w_rim * (cp[last] * w_end)

    pl.when(has_left)(lambda: to_left().wait_send())
    pl.when(has_right)(lambda: to_right().wait_send())
    pl.when(has_right)(lambda: to_left().wait_recv())
    pl.when(has_left)(lambda: to_right().wait_recv())
    col_mass = density[0, 0] * cols_t[0, 0]
    for e in range(1, elements):
        col_mass = col_mass + density[0, e] * cols_t[e, 0]
    col_mass = col_mass + jnp.where(row == 0, w_end * dens_in[...], 0.0)
    rim_mass = w_end * (density[0, last] + halo_in[2 * comps])
    inv_main = [step_scale / (float(weights[a]) * col_mass) for a in range(nr)]
    inv_rim = step_scale / (jnp.where(row < nr, w_rim, 1.0) * rim_mass)
    inv_rim = jnp.where(has_right, inv_rim, 0.0)

    rim = halo_in[0:comps]
    rim_before = rim - halo_in[comps : 2 * comps]
    before = [u[a] - v[a] for a in range(nr)]

    def swap(x):
        axis = x.ndim - 1
        return jnp.where(even, pltpu.roll(x, width - 1, axis), -pltpu.roll(x, 1, axis))

    def pair(x, factor):
        return jnp.stack(
            [factor * swap(x[2]), jnp.zeros((cols, width), jnp.float32), -factor * swap(x[0])]
        )

    def left_force(step):
        return remote(fl_out.at[step], fr_in.at[step], f_s.at[0, step], f_r.at[0, step], (o - 1, q))

    def right_force(step):
        return remote(fr_out.at[step], fl_in.at[step], f_s.at[1, step], f_r.at[1, step], (o + 1, q))

    for step in range(STEPS):
        forces, rim_force = [], jnp.zeros((comps, cols, width), jnp.float32)
        for a in range(nr):
            w_a = float(weights[a])
            colat = c_rim * rim[:, a : a + 1, :] + c_colat[0] * u[a]
            for d in range(1, cols):
                colat = colat + c_colat[d] * pltpu.roll(u[a], d, 1)
            radial = float(stiffness[a, 0]) * u[0]
            for i in range(1, nr):
                radial = radial + float(stiffness[a, i]) * u[i]
            force = pair(u[a], w_a * c_pair) - (
                c_radial * radial + w_a * (colat + c_hoop * u[a])
            )
            forces.append(force)
            ending = jnp.sum(c_rim * u[a], axis=1, keepdims=True)
            rim_force = jnp.where((row == a)[None], -w_a * ending, rim_force)
        rim_force = rim_force + pair(rim, r_pair)
        for d in range(cols):
            rim_force = rim_force - r_radial[d] * (pltpu.roll(rim, d, 1) if d else rim)
        fl_out[step] = first_column(forces)
        fr_out[step] = rim_force
        pl.when(has_left)(lambda: left_force(step).start())
        pl.when(has_right)(lambda: right_force(step).start())
        ahead = [2.0 * u[a] - before[a] + inv_main[a] * forces[a] for a in range(nr)]
        if step == 0:
            pl.loop(1, n)(lambda h: meta_copy(h).wait_send())
            pl.loop(1, n)(lambda h: meta_copy(h).wait_recv())
            mix[...] = jnp.zeros_like(mix)
            wanted = lax.broadcasted_iota(jnp.int32, (cells, points), 0)
            wanted = ((wanted % depth) * (cells // depth) + wanted // depth).astype(jnp.float32)
            upper = lane >= slot

            def horner(x, at, count):
                total = lanes_t[at + count - 1 : at + count, :]
                for p in range(count - 2, -1, -1):
                    total = total * x + lanes_t[at + p : at + p + 1, :]
                return total

            def block_mix(i):
                xi, eta = as_column(meta[i, 0:1, :]), as_column(meta[i, 1:2, :])
                spot, factor = as_column(meta[i, 2:3, :]), as_column(meta[i, 4:5, :])
                xi = jnp.broadcast_to(xi, (points, width))
                eta = jnp.broadcast_to(eta, (points, width))
                l_xi, s_xi = horner(xi, 0, 5), horner(xi, 5, 4)
                l_eta, s_eta = horner(eta, 9, 5), horner(eta, 14, 4)
                for e in range(1, elements):
                    here = spot == float(e)
                    l_eta = jnp.where(here, horner(eta, 9 + 9 * e, 5), l_eta)
                    s_eta = jnp.where(here, horner(eta, 14 + 9 * e, 4), s_eta)
                mine = meta[i, 3:4, 0:points] == o.astype(jnp.float32)
                chosen = jnp.where(mine & (meta[i, 5:6, 0:points] == wanted), 1.0, 0.0)
                chosen = chosen.astype(jnp.bfloat16)
                parts = []
                for table in (s_xi * l_eta, l_xi * s_eta, factor * (l_xi * l_eta)):
                    high, low = halves(table)
                    parts.append(dot(chosen, high) + dot(chosen, low))
                return jnp.concatenate(parts, axis=0)

            @pl.loop(0, n // 2)
            def _(j):
                first, second = block_mix(2 * j), pltpu.roll(block_mix(2 * j + 1), slot, 1)
                mix[j] = mix[j] + first + jnp.where(upper, second, 0.0)
                mix[j + 1] = mix[j + 1] + jnp.where(upper, 0.0, second)

        pl.when(has_left)(lambda: left_force(step).wait_send())
        pl.when(has_right)(lambda: right_force(step).wait_send())
        pl.when(has_right)(lambda: left_force(step).wait_recv())
        pl.when(has_left)(lambda: right_force(step).wait_recv())
        from_left = fl_in[step]
        for a in range(nr):
            ahead[a] = ahead[a] + jnp.where(
                (row == 0)[None], inv_main[a] * from_left[:, a : a + 1, :], 0.0
            )
        rim_ahead = 2.0 * rim - rim_before + inv_rim * (rim_force + fr_in[step])
        rim_ahead = jnp.where(has_right, rim_ahead, 0.0)
        before, u, rim_before, rim = u, ahead, rim, rim_ahead

    for a in range(nr):
        gathered[o, :, a * cols : (a + 1) * cols, :] = u[a]
    lo, hi, groups = lax.rem(o, 2), lax.div(o, 2), n // 2
    partner = hi * 2 + 1 - lo

    def far(h):
        block = gathered.at[o, :, 0:nodes, :]
        to = lax.rem(hi + h, groups) * 2 + lo
        return remote(block, block, ga_s.at[h], ga_r.at[h], (to, q))

    def near(h):
        block = gathered.at[lax.rem(hi + groups - h, groups) * 2 + lo, :, 0:nodes, :]
        return remote(block, block, gb_s.at[h], gb_r.at[h], (partner, q))

    pl.loop(1, groups)(lambda h: far(h).start())
    near(0).start()
    for a in range(nr):
        out_u[:, a] = u[a]
    for copy in basis_copies:
        copy.wait()

    @pl.loop(1, groups)
    def _(h):
        far(h).wait_recv()
        near(h).start()

    for h in range(1, az):
        adj_copy(h).wait_send()
        adj_copy(h).wait_recv()
    pl.loop(0, groups)(lambda h: near(h).wait_recv())

    def block_of(j, s):
        return jnp.concatenate([gathered[2 * j, s], gathered[2 * j + 1, s]], axis=0)

    def add_pair(j, total):
        left = halves(mix[j])
        return tuple(total[s] + dot3(left, halves(block_of(j, s))) for s in range(comps))

    zero = jnp.zeros((3 * cells, width), jnp.float32)
    coefs = lax.fori_loop(0, groups, add_pair, (zero,) * comps)
    rows = []
    for s in range(comps):
        rows.append(coefs[s][0 : 2 * cells])
        rows.append(swap(coefs[s][2 * cells :]) * ratio)
    split = halves(jnp.concatenate(rows, axis=0))
    raw = []
    for h in range(az):
        r = lax.rem(q + h, az)
        samples = dot3(split, (bh[r], bl[r]))
        total = jnp.zeros((cells, width), jnp.float32)
        for g in range(3 * comps):
            values = adjoint[g] if h == 0 else adj_all[h, g]
            total = total + samples[g * cells : (g + 1) * cells] * values
        raw.append(total)
    raw = jnp.concatenate(raw, axis=1)
    whole = az * width
    for h in range(az):
        at = slice(h * width, (h + 1) * width)
        face_out[0, h] = raw[0:depth, at]
        face_out[1, h] = raw[cells - depth :, at]

    def face_left(h):
        return remote(
            face_out.at[0, h], face_in.at[1, h], face_s.at[0, h], face_r.at[0, h],
            (o - 1, lax.rem(q + h, az)),
        )

    def face_right(h):
        return remote(
            face_out.at[1, h], face_in.at[0, h], face_s.at[1, h], face_r.at[1, h],
            (o + 1, lax.rem(q + h, az)),
        )

    for h in range(az):
        pl.when(has_left)(lambda: face_left(h).start())
        pl.when(has_right)(lambda: face_right(h).start())
    level = lax.broadcasted_iota(jnp.int32, (cells, whole), 0)
    level_in = level % depth
    around = pltpu.roll(raw, 1, 1) + pltpu.roll(raw, whole - 1, 1)
    around = around + jnp.where(level_in > 0, pltpu.roll(raw, 1, 0), 0.0)
    around = around + jnp.where(level_in < depth - 1, pltpu.roll(raw, cells - 1, 0), 0.0)
    around = around + jnp.where(level >= depth, pltpu.roll(raw, depth, 0), 0.0)
    around = around + jnp.where(level < cells - depth, pltpu.roll(raw, cells - depth, 0), 0.0)
    smooth = (1.0 - 6.0 * smooth_rate) * raw + smooth_rate * around

    def part_copy(h):
        return remote(
            part_out.at[h], part_in.at[h], part_s.at[h], part_r.at[h], (o, lax.rem(q + h, az))
        )

    for h in range(1, az):
        part_out[h] = smooth[:, h * width : (h + 1) * width]
        part_copy(h).start()
    result = smooth[:, 0:width]
    for h in range(1, az):
        part_copy(h).wait_recv()
        result = result + part_in[h]
    for h in range(az):
        pl.when(has_right)(lambda: face_left(h).wait_recv())
        pl.when(has_left)(lambda: face_right(h).wait_recv())
    below, above = face_in[0, 0], face_in[1, 0]
    for h in range(1, az):
        below, above = below + face_in[0, h], above + face_in[1, h]
    out_k[...] = result
    out_k[0:depth] = result[0:depth] + smooth_rate * below
    out_k[cells - depth :] = out_k[cells - depth :] + smooth_rate * above

    for h in range(1, az):
        part_copy(h).wait_send()
    for h in range(az):
        pl.when(has_left)(lambda: face_left(h).wait_send())
        pl.when(has_right)(lambda: face_right(h).wait_send())
    pl.loop(1, groups)(lambda h: far(h).wait_send())
    pl.loop(0, groups)(lambda h: near(h).wait_send())


def on_device(
    n, az, disp, vel, modulus, hoop, coupling, density, orders, element, local, scale, owner, cell,
    adjoint,
):
    comps, nr, cols, width = disp.shape
    elements, points = modulus.shape[1], owner.shape[0]
    layers, lats, phi_width = adjoint.shape[1:]
    cells = layers * lats
    turned = jnp.swapaxes(adjoint, 1, 2).reshape(9, cells, phi_width)
    high, low = basis_tables(az, width, phi_width)
    vm, sm = pl.BlockSpec(memory_space=pltpu.VMEM), pl.BlockSpec(memory_space=pltpu.SMEM)
    anywhere = pl.BlockSpec(memory_space=pl.ANY)
    slot = width // 2
    f32, dma = jnp.float32, pltpu.SemaphoreType.DMA
    buf = lambda *shape: pltpu.VMEM(shape, f32)
    final, smoothed = pl.pallas_call(
        functools.partial(kernel, n, az),
        out_shape=(
            jax.ShapeDtypeStruct(disp.shape, f32),
            jax.ShapeDtypeStruct((cells, phi_width), f32),
        ),
        in_specs=[vm, vm, sm, sm, sm, sm, sm] + [vm] * 6 + [anywhere] * 2 + [vm] * 3,
        out_specs=(vm, vm),
        scratch_shapes=[
            buf(2 * comps + 1, cols, width), buf(2 * comps + 1, cols, width),
            buf(cols, width), buf(cols, width),
            buf(STEPS, comps, cols, width), buf(STEPS, comps, cols, width),
            buf(STEPS, comps, cols, width), buf(STEPS, comps, cols, width),
            buf(n, 8, width), buf(n, comps, slot, width), buf(n // 2 + 1, 3 * cells, width),
            buf(az, 9, cells, phi_width),
            pltpu.VMEM((az, width, phi_width), jnp.bfloat16),
            pltpu.VMEM((az, width, phi_width), jnp.bfloat16),
            buf(az, cells, phi_width), buf(az, cells, phi_width),
            buf(2, az, layers, phi_width), buf(2, az, layers, phi_width),
            dma, dma, dma, dma, dma((2, STEPS)), dma((2, STEPS)), dma((n,)), dma((n,)),
            dma((az,)), dma((az,)), dma((n,)), dma((n,)), dma((n,)), dma((n,)),
            dma((az,)), dma((az,)), dma((2, az)), dma((2, az)), dma((2,)),
        ],
        compiler_params=pltpu.CompilerParams(
            collective_id=0, has_side_effects=True, vmem_limit_bytes=40 * 1024 * 1024
        ),
    )(
        disp, vel, modulus, hoop, coupling, density, orders, element, local,
        scale.reshape(1, points), owner, cell.reshape(1, points), turned,
        jnp.asarray(high), jnp.asarray(low),
        jnp.asarray(lane_table(elements, cols, width)),
        jnp.asarray(column_table(elements, cols, width)),
        jnp.asarray(rim_table(cols, width)),
    )
    return final, jnp.swapaxes(smoothed.reshape(lats, layers, phi_width), 0, 1)


def solution(mesh):
    field = P(None, None, "mer", "az")
    placed = (
        field, field, P(None, "mer"), P(None, "mer"), P(None, "mer"), P(None, "mer"),
        P(None, "mer"), P("mer", None), P("mer", None), P("mer"), P("mer", None), P("mer"), field,
    )
    return jax.shard_map(
        functools.partial(on_device, mesh.shape["mer"], mesh.shape["az"]),
        mesh=mesh,
        in_specs=placed,
        out_specs=(field, P(None, "mer", "az")),
        check_vma=False,
    )
```

```python
import functools
import math

import jax
import jax.numpy as jnp
import ml_dtypes
import numpy as np
from jax import lax
from jax.experimental import pallas as pl
from jax.experimental.pallas import tpu as pltpu
from jax.sharding import PartitionSpec as P

ORDERS = 256
STEPS = 3
step_scale = 0.015
smooth_rate = 0.125
MESH = pl.DeviceIdType.MESH


def gll_tables():
    nodes = np.array([-1.0, -math.sqrt(3.0 / 7.0), 0.0, math.sqrt(3.0 / 7.0), 1.0])
    weights = np.array([0.1, 49.0 / 90.0, 32.0 / 45.0, 49.0 / 90.0, 0.1])
    monomials = np.zeros((5, 5))
    for j in range(5):
        poly = np.array([1.0])
        for l in range(5):
            if l != j:
                poly = np.convolve(poly, np.array([1.0, -nodes[l]]) / (nodes[j] - nodes[l]))
        monomials[j] = poly[::-1]
    slopes = monomials[:, 1:] * np.arange(1, 5)
    derivative = np.array(
        [[sum(slopes[j, p] * nodes[i] ** p for p in range(4)) for j in range(5)] for i in range(5)]
    )
    stiffness = derivative.T @ np.diag(weights) @ derivative
    return weights, monomials, slopes, stiffness


def point_table(elements, cols, lanes):
    _, monomials, slopes, _ = gll_tables()
    both = np.concatenate([monomials, slopes], axis=1)
    table = np.zeros((1 + elements, 9, cols, lanes), np.float32)
    table[0, :, 0:5] = both.T[:, :, None]
    for e in range(elements):
        for c in range(cols):
            if 0 <= c - 4 * e <= 4:
                table[1 + e, :, c] = both[c - 4 * e][:, None]
    return table.reshape(-1, cols, lanes)


def column_table(elements, cols, lanes):
    weights, _, _, stiffness = gll_tables()
    table = np.zeros((elements, cols + 2, cols, lanes), np.float32)
    for e in range(elements):
        for c in range(cols):
            b = c - 4 * e
            if not 0 <= b <= 4:
                continue
            table[e, 0, c] = weights[b]
            for d in range(cols):
                other = (c - d) % cols - 4 * e
                if 0 <= other <= 4:
                    table[e, 1 + d, c] = stiffness[b, other]
            if cols - 4 * e == 4:
                table[e, cols + 1, c] = stiffness[b, 4]
    return table


def rim_table(cols, lanes):
    _, _, _, stiffness = gll_tables()
    table = np.zeros((cols, cols, lanes), np.float32)
    for d in range(cols):
        for a in range(5):
            other = (a - d) % cols
            if other <= 4:
                table[d, a] = stiffness[a, other]
    return table


def basis_tables(az_count, width, phi_width):
    coefs, phis = az_count * width, az_count * phi_width
    k, j = np.arange(coefs)[:, None], np.arange(phis)[None, :]
    angles = (k // 2) * j % (2 * ORDERS) * (2.0 * math.pi / (2 * ORDERS))
    basis = np.where(k % 2 == 0, np.cos(angles), np.sin(angles)) / math.sqrt(ORDERS)
    basis = basis.reshape(az_count, width, az_count, phi_width)
    turned = [
        np.concatenate([basis[q, :, (q + h) % az_count] for h in range(az_count)], axis=1)
        for q in range(az_count)
    ]
    basis = np.stack(turned).astype(np.float32)
    high = basis.astype(ml_dtypes.bfloat16)
    low = (basis - high.astype(np.float32)).astype(ml_dtypes.bfloat16)
    return np.concatenate([high, high, low], axis=1)


def halves(x):
    high = x.astype(jnp.bfloat16)
    return high, (x - high.astype(jnp.float32)).astype(jnp.bfloat16)


def dot(x, y):
    return jnp.dot(x, y, preferred_element_type=jnp.float32)


def left_parts(x):
    high, low = halves(x)
    return jnp.concatenate([high, low, high], axis=1)


def right_parts(x):
    high, low = halves(x)
    return jnp.concatenate([high, high, low], axis=0)


def kernel(
    n, az, disp_a, vel_a, modulus_a, hoop_a, coupling_a, density_a, orders_a, element_a, local_a,
    scale_a, owner_a, cell_a, adjoint_a, basis_a, tiles_a, out_u, out_k,
    disp, vel, modulus, hoop, coupling, density, orders, element, local, scale, owner, cell,
    adjoint, basis, tiles, final,
    halo_out, halo_in, dens_out, dens_in, fl_out, fr_out, fl_in, fr_in, meta, gathered, mix,
    adj_all, part_out, part_in, face_out, face_in,
    halo_s, halo_r, dens_s, dens_r, f_s, f_r, meta_s, meta_r, adj_s, adj_r, ga_s, ga_r, gb_s, gb_r,
    part_s, part_r, face_s, face_r, in_s, out_s,
):
    o, q = lax.axis_index("mer"), lax.axis_index("az")
    comps, nr, cols, width = disp.shape
    elements = modulus.shape[1]
    points = owner.shape[1]
    slot = gathered.shape[2]
    nodes = nr * cols
    cells = adjoint.shape[1]
    depth = face_in.shape[2]
    lats = cells // depth
    weights, _, _, stiffness = gll_tables()
    has_left, has_right = o > 0, o < n - 1
    pairs = [
        (disp_a, disp), (vel_a, vel), (modulus_a, modulus), (hoop_a, hoop), (coupling_a, coupling),
        (density_a, density), (orders_a, orders), (element_a, element), (local_a, local),
        (scale_a, scale), (owner_a, owner), (cell_a, cell), (tiles_a, tiles), (adjoint_a, adjoint),
        (basis_a.at[q], basis),
    ]
    fetches = [pltpu.make_async_copy(src, dst, in_s.at[i]) for i, (src, dst) in enumerate(pairs)]
    for fetch in fetches:
        fetch.start()

    halo_in[...] = jnp.zeros_like(halo_in)
    dens_in[...] = jnp.zeros_like(dens_in)
    fl_in[...] = jnp.zeros_like(fl_in)
    fr_in[...] = jnp.zeros_like(fr_in)
    face_in[...] = jnp.zeros_like(face_in)
    gathered[:, :, nodes:, :] = jnp.zeros((n, comps, slot - nodes, width), jnp.float32)

    barrier = pltpu.get_barrier_semaphore()

    @pl.loop(1, n)
    def _(h):
        pl.semaphore_signal(barrier, inc=1, device_id=(lax.rem(o + h, n), q), device_id_type=MESH)

    for h in range(1, az):
        r = lax.rem(q + h, az)
        pl.semaphore_signal(barrier, inc=1, device_id=(o, r), device_id_type=MESH)

        @pl.when(has_left)
        def _():
            pl.semaphore_signal(barrier, inc=1, device_id=(o - 1, r), device_id_type=MESH)

        @pl.when(has_right)
        def _():
            pl.semaphore_signal(barrier, inc=1, device_id=(o + 1, r), device_id_type=MESH)

    for fetch in fetches[:-2]:
        fetch.wait()

    row = lax.broadcasted_iota(jnp.int32, (cols, width), 0)
    lane = lax.broadcasted_iota(jnp.int32, (1, width), 1)
    u = [disp[:, a] for a in range(nr)]
    v = [vel[:, a] for a in range(nr)]

    def first_column(values):
        total = jnp.zeros((comps, cols, width), jnp.float32)
        for a in range(nr):
            total = jnp.where((row == a)[None], values[a][:, 0:1, :], total)
        return total

    halo_out[0:comps] = first_column(u)
    halo_out[comps : 2 * comps] = first_column(v)
    halo_out[2 * comps] = jnp.broadcast_to(density[0:1, 0:1], (cols, width))
    dens_out[...] = jnp.broadcast_to(
        density[0:1, elements - 1 : elements], (cols, width)
    )
    spare = jnp.zeros((1, width - points), jnp.float32) if width > points else None

    def wide(line):
        return line if spare is None else jnp.concatenate([line, spare], axis=1)

    meta[o] = jnp.concatenate(
        [
            wide(local[0:1, :]),
            wide(local[1:2, :]),
            wide((element[1:2, :] % elements).astype(jnp.float32)),
            wide(owner[...].astype(jnp.float32)),
            wide(scale[...]),
            wide(cell[...].astype(jnp.float32)),
            jnp.zeros((2, width), jnp.float32),
        ],
        axis=0,
    )

    pl.semaphore_wait(
        barrier,
        n - 1 + (az - 1) * (1 + has_left.astype(jnp.int32) + has_right.astype(jnp.int32)),
    )

    def remote(src, dst, send, recv, device):
        return pltpu.make_async_remote_copy(
            src_ref=src, dst_ref=dst, send_sem=send, recv_sem=recv,
            device_id=device, device_id_type=MESH,
        )

    to_left = lambda: remote(halo_out, halo_in, halo_s, halo_r, (o - 1, q))
    to_right = lambda: remote(dens_out, dens_in, dens_s, dens_r, (o + 1, q))
    pl.when(has_left)(lambda: to_left().start())
    pl.when(has_right)(lambda: to_right().start())

    def meta_copy(h):
        return remote(meta.at[o], meta.at[o], meta_s.at[h], meta_r.at[h], (lax.rem(o + h, n), q))

    pl.loop(1, n)(lambda h: meta_copy(h).start())

    def adj_copy(h):
        return remote(
            adjoint, adj_all.at[h], adj_s.at[h], adj_r.at[h], (o, lax.rem(q + az - h, az))
        )

    fetches[-2].wait()
    for h in range(1, az):
        adj_copy(h).start()

    order = (q * width + lane) // 2
    ratio = order.astype(jnp.float32) / ORDERS
    even = (lane % 2 == 0)
    one = lambda ref, e: ref[0:1, e : e + 1]
    keep = [jnp.where(order < one(orders, e), 1.0, 0.0) for e in range(elements)]
    mod = [one(modulus, e) * keep[e] for e in range(elements)]
    hp = [one(hoop, e) * keep[e] * (ratio * ratio) for e in range(elements)]
    cp = [one(coupling, e) * keep[e] * ratio for e in range(elements)]
    points_at = 0
    cols_at = 9 * (1 + elements)
    rim_at = cols_at + elements * (cols + 2)
    cols_t = lambda e, which: tiles[cols_at + e * (cols + 2) + which]
    last = elements - 1
    w_end = float(weights[4])

    def blend(per_element, which):
        total = per_element[0] * cols_t(0, which)
        for e in range(1, elements):
            total = total + per_element[e] * cols_t(e, which)
        return total

    c_radial, c_hoop, c_pair = blend(mod, 0), blend(hp, 0), blend(cp, 0)
    c_colat = [blend(mod, 1 + d) for d in range(cols)]
    c_rim = mod[last] * cols_t(last, cols + 1)
    w_rim = jnp.zeros((cols, width), jnp.float32)
    for a in range(nr):
        w_rim = jnp.where(row == a, float(weights[a]), w_rim)
    r_radial = [mod[last] * w_end * tiles[rim_at + d] for d in range(cols)]
    r_radial[0] = r_radial[0] + w_rim * (
        mod[last] * float(stiffness[4, 4]) + hp[last] * w_end
    )
    r_pair = w_rim * (cp[last] * w_end)

    pl.when(has_right)(lambda: to_left().wait_recv())
    pl.when(has_left)(lambda: to_right().wait_recv())
    col_mass = one(density, 0) * cols_t(0, 0)
    for e in range(1, elements):
        col_mass = col_mass + one(density, e) * cols_t(e, 0)
    col_mass = col_mass + jnp.where(row == 0, w_end * dens_in[...], 0.0)
    rim_mass = w_end * (one(density, last) + halo_in[2 * comps])
    inv_main = [step_scale / (float(weights[a]) * col_mass) for a in range(nr)]
    inv_rim = step_scale / (jnp.where(row < nr, w_rim, 1.0) * rim_mass)
    inv_rim = jnp.where(has_right, inv_rim, 0.0)

    rim = halo_in[0:comps]
    rim_before = rim - halo_in[comps : 2 * comps]
    before = [u[a] - v[a] for a in range(nr)]

    def swap(x):
        axis = x.ndim - 1
        return jnp.where(even, pltpu.roll(x, width - 1, axis), -pltpu.roll(x, 1, axis))

    def pair(x, factor):
        return jnp.stack(
            [factor * swap(x[2]), jnp.zeros((cols, width), jnp.float32), -factor * swap(x[0])]
        )

    def left_force(step):
        return remote(fl_out.at[step], fr_in.at[step], f_s.at[0, step], f_r.at[0, step], (o - 1, q))

    def right_force(step):
        return remote(fr_out.at[step], fl_in.at[step], f_s.at[1, step], f_r.at[1, step], (o + 1, q))

    wanted = lax.broadcasted_iota(jnp.int32, (cells, width), 0).astype(jnp.float32)
    upper = lane >= slot
    blank = jnp.zeros((slot - nodes, width), jnp.float32)
    _, monomials, slopes, _ = gll_tables()

    def horner(x, coefs):
        total = coefs[-1]
        for coef in coefs[-2::-1]:
            total = total * x + coef
        return total

    def tile_horner(x, at, count):
        return horner(x, [tiles[points_at + at + p] for p in range(count)])

    def block_mix(i):
        line = lambda k: meta[i, k : k + 1, :]
        xi, eta, spot, factor = line(0), line(1), line(2), line(4)
        l_xi, s_xi = tile_horner(xi, 0, 5), tile_horner(xi, 5, 4)
        l_eta, s_eta = tile_horner(eta, 9, 5), tile_horner(eta, 14, 4)
        for e in range(1, elements):
            here = spot == float(e)
            l_eta = jnp.where(here, tile_horner(eta, 9 + 9 * e, 5), l_eta)
            s_eta = jnp.where(here, tile_horner(eta, 14 + 9 * e, 4), s_eta)
        at_end = spot == float(elements - 1)
        l_end = jnp.where(at_end, horner(eta, [float(x) for x in monomials[4]]), 0.0)
        s_end = jnp.where(at_end, horner(eta, [float(x) for x in slopes[4]]), 0.0)
        parts = []
        for x, y, y_end in (
            (s_xi, l_eta, l_end), (l_xi, s_eta, s_end), (factor * l_xi, l_eta, l_end)
        ):
            parts += [x[a : a + 1, :] * y for a in range(nr)] + [blank]
            end = x * y_end
            parts += [jnp.where(row == 0, end[a : a + 1, :], 0.0) for a in range(nr)] + [blank]
        high, low = halves(jnp.concatenate(parts, axis=0))
        chosen = (line(3) == o.astype(jnp.float32)) & (line(5) == wanted)
        chosen = chosen & (lane < points)
        chosen = jnp.where(chosen, 1.0, 0.0).astype(jnp.bfloat16)
        taken = lax.dot_general(
            jnp.concatenate([chosen, chosen], axis=1),
            jnp.concatenate([high, low], axis=1),
            (((1,), (1,)), ((), ())),
            preferred_element_type=jnp.float32,
        )
        return jnp.concatenate([taken[:, t * width : (t + 1) * width] for t in range(3)], axis=0)

    def mix_blocks(start, stop):
        @pl.loop(start, stop)
        def _(j):
            first, second = block_mix(2 * j), pltpu.roll(block_mix(2 * j + 1), slot, 1)
            mix[j] = mix[j] + first + jnp.where(upper, second, 0.0)
            mix[j + 1] = mix[j + 1] + jnp.where(upper, 0.0, second)

    for step in range(STEPS):
        forces, rim_force = [], jnp.zeros((comps, cols, width), jnp.float32)
        for a in range(nr):
            w_a = float(weights[a])
            colat = c_rim * rim[:, a : a + 1, :] + c_colat[0] * u[a]
            for d in range(1, cols):
                colat = colat + c_colat[d] * pltpu.roll(u[a], d, 1)
            radial = float(stiffness[a, 0]) * u[0]
            for i in range(1, nr):
                radial = radial + float(stiffness[a, i]) * u[i]
            force = pair(u[a], w_a * c_pair) - (
                c_radial * radial + w_a * (colat + c_hoop * u[a])
            )
            forces.append(force)
            ending = jnp.sum(c_rim * u[a], axis=1, keepdims=True)
            rim_force = jnp.where((row == a)[None], -w_a * ending, rim_force)
        rim_force = rim_force + pair(rim, r_pair)
        for d in range(cols):
            rim_force = rim_force - r_radial[d] * (pltpu.roll(rim, d, 1) if d else rim)
        fl_out[step] = first_column(forces)
        fr_out[step] = rim_force
        pl.when(has_left)(lambda: left_force(step).start())
        pl.when(has_right)(lambda: right_force(step).start())
        ahead = [2.0 * u[a] - before[a] + inv_main[a] * forces[a] for a in range(nr)]
        if step == 0:
            pl.loop(1, n)(lambda h: meta_copy(h).wait_recv())
            mix[...] = jnp.zeros_like(mix)
        mix_blocks(n // 2 * step // STEPS, n // 2 * (step + 1) // STEPS)
        pl.when(has_right)(lambda: left_force(step).wait_recv())
        pl.when(has_left)(lambda: right_force(step).wait_recv())
        from_left = fl_in[step]
        for a in range(nr):
            ahead[a] = ahead[a] + jnp.where(
                (row == 0)[None], inv_main[a] * from_left[:, a : a + 1, :], 0.0
            )
        rim_ahead = 2.0 * rim - rim_before + inv_rim * (rim_force + fr_in[step])
        rim_ahead = jnp.where(has_right, rim_ahead, 0.0)
        before, u, rim_before, rim = u, ahead, rim, rim_ahead

    for a in range(nr):
        gathered[o, :, a * cols : (a + 1) * cols, :] = u[a]
    lo, hi, groups = lax.rem(o, 2), lax.div(o, 2), n // 2
    partner = hi * 2 + 1 - lo

    def far(h):
        block = gathered.at[o, :, 0:nodes, :]
        to = lax.rem(hi + h, groups) * 2 + lo
        return remote(block, block, ga_s.at[h], ga_r.at[h], (to, q))

    def near(h):
        block = gathered.at[lax.rem(hi + groups - h, groups) * 2 + lo, :, 0:nodes, :]
        return remote(block, block, gb_s.at[h], gb_r.at[h], (partner, q))

    pl.loop(1, groups)(lambda h: far(h).start())
    near(0).start()
    for a in range(nr):
        final[:, a] = u[a]
    final_copy = pltpu.make_async_copy(final, out_u, out_s)
    final_copy.start()

    def add_group(h, total):
        near(h).wait_recv()
        j = lax.rem(hi + groups - h, groups)
        block = [
            jnp.concatenate([gathered[2 * j, s], gathered[2 * j + 1, s]], axis=0)
            for s in range(comps)
        ]
        return total + dot(left_parts(mix[j]), right_parts(jnp.concatenate(block, axis=1)))

    def next_group(h, total):
        far(h).wait_recv()
        near(h).start()
        return add_group(h - 1, total)

    coefs = lax.fori_loop(
        1, groups, next_group, jnp.zeros((3 * cells, comps * width), jnp.float32)
    )
    coefs = add_group(groups - 1, coefs)
    fetches[-1].wait()
    for h in range(1, az):
        adj_copy(h).wait_recv()
    coefs = [coefs[:, s * width : (s + 1) * width] for s in range(comps)]
    rows = []
    for s in range(comps):
        rows.append(coefs[s][0 : 2 * cells])
        rows.append(swap(coefs[s][2 * cells :]) * ratio)
    samples = dot(left_parts(jnp.concatenate(rows, axis=0)), basis[...])
    raw = []
    for h in range(az):
        total = jnp.zeros((cells, width), jnp.float32)
        for g in range(3 * comps):
            values = adjoint[g] if h == 0 else adj_all[h, g]
            at = samples[g * cells : (g + 1) * cells, h * width : (h + 1) * width]
            total = total + at * values
        raw.append(total)
    raw = jnp.concatenate(raw, axis=1)
    whole = az * width
    tile_lat = lax.broadcasted_iota(jnp.int32, (depth, width), 0) % lats
    for h in range(az):
        low_face = jnp.zeros((depth, width), jnp.float32)
        high_face = jnp.zeros((depth, width), jnp.float32)
        for i in range(cells // depth):
            tile = raw[i * depth : (i + 1) * depth, h * width : (h + 1) * width]
            first = pltpu.roll(jnp.where(tile_lat == 0, tile, 0.0), i, 0) if i else (
                jnp.where(tile_lat == 0, tile, 0.0)
            )
            low_face = low_face + first
            turn = (i + depth - (lats - 1)) % depth
            final_row = jnp.where(tile_lat == lats - 1, tile, 0.0)
            high_face = high_face + (pltpu.roll(final_row, turn, 0) if turn else final_row)
        face_out[0, h] = low_face
        face_out[1, h] = high_face

    def face_left(h):
        return remote(
            face_out.at[0, h], face_in.at[1, h], face_s.at[0, h], face_r.at[0, h],
            (o - 1, lax.rem(q + h, az)),
        )

    def face_right(h):
        return remote(
            face_out.at[1, h], face_in.at[0, h], face_s.at[1, h], face_r.at[1, h],
            (o + 1, lax.rem(q + h, az)),
        )

    for h in range(az):
        pl.when(has_left)(lambda: face_left(h).start())
        pl.when(has_right)(lambda: face_right(h).start())
    level = lax.broadcasted_iota(jnp.int32, (cells, whole), 0)
    lat = level % lats
    around = pltpu.roll(raw, 1, 1) + pltpu.roll(raw, whole - 1, 1)
    around = around + jnp.where(lat > 0, pltpu.roll(raw, 1, 0), 0.0)
    around = around + jnp.where(lat < lats - 1, pltpu.roll(raw, cells - 1, 0), 0.0)
    around = around + jnp.where(level >= lats, pltpu.roll(raw, lats, 0), 0.0)
    around = around + jnp.where(level < cells - lats, pltpu.roll(raw, cells - lats, 0), 0.0)
    smooth = (1.0 - 6.0 * smooth_rate) * raw + smooth_rate * around

    def part_copy(h):
        return remote(
            part_out.at[h], part_in.at[h], part_s.at[h], part_r.at[h], (o, lax.rem(q + h, az))
        )

    for h in range(1, az):
        part_out[h] = smooth[:, h * width : (h + 1) * width]
        part_copy(h).start()
    result = smooth[:, 0:width]
    for h in range(1, az):
        part_copy(h).wait_recv()
        result = result + part_in[h]
    for h in range(az):
        pl.when(has_right)(lambda: face_left(h).wait_recv())
        pl.when(has_left)(lambda: face_right(h).wait_recv())
    below, above = face_in[0, 0], face_in[1, 0]
    for h in range(1, az):
        below, above = below + face_in[0, h], above + face_in[1, h]
    for i in range(cells // depth):
        turn = (lats - 1 - i) % depth
        first = pltpu.roll(below, (depth - i) % depth, 0) if i else below
        final_row = pltpu.roll(above, turn, 0) if turn else above
        extra = jnp.where(tile_lat == 0, first, 0.0) + jnp.where(
            tile_lat == lats - 1, final_row, 0.0
        )
        at = slice(i * depth, (i + 1) * depth)
        out_k[at] = result[at] + smooth_rate * extra

    final_copy.wait()
    pl.when(has_left)(lambda: to_left().wait_send())
    pl.when(has_right)(lambda: to_right().wait_send())
    pl.loop(1, n)(lambda h: meta_copy(h).wait_send())
    for step in range(STEPS):
        pl.when(has_left)(lambda: left_force(step).wait_send())
        pl.when(has_right)(lambda: right_force(step).wait_send())
    for h in range(1, az):
        adj_copy(h).wait_send()
    for h in range(1, az):
        part_copy(h).wait_send()
    for h in range(az):
        pl.when(has_left)(lambda: face_left(h).wait_send())
        pl.when(has_right)(lambda: face_right(h).wait_send())
    pl.loop(1, groups)(lambda h: far(h).wait_send())
    pl.loop(0, groups)(lambda h: near(h).wait_send())


def on_device(
    n, az, disp, vel, modulus, hoop, coupling, density, orders, element, local, scale, owner, cell,
    adjoint,
):
    comps, nr, cols, width = disp.shape
    elements, points = modulus.shape[1], owner.shape[0]
    layers, lats, phi_width = adjoint.shape[1:]
    cells = layers * lats
    assert nr == 5 and cols == 4 * elements and layers == 8 and layers % lats == 0
    assert points <= width and width == phi_width
    tiles = np.concatenate(
        [
            point_table(elements, cols, width),
            column_table(elements, cols, width).reshape(-1, cols, width),
            rim_table(cols, width),
        ]
    )
    basis = basis_tables(az, width, phi_width)
    vm = pl.BlockSpec(memory_space=pltpu.VMEM)
    anywhere = pl.BlockSpec(memory_space=pl.ANY)
    slot = width // 2
    f32, dma = jnp.float32, pltpu.SemaphoreType.DMA
    buf = lambda *shape: pltpu.VMEM(shape, f32)
    ints = lambda *shape: pltpu.VMEM(shape, jnp.int32)
    final, smoothed = pl.pallas_call(
        functools.partial(kernel, n, az),
        out_shape=(
            jax.ShapeDtypeStruct(disp.shape, f32),
            jax.ShapeDtypeStruct((cells, phi_width), f32),
        ),
        in_specs=[anywhere] * 15,
        out_specs=(anywhere, vm),
        scratch_shapes=[
            buf(*disp.shape), buf(*vel.shape),
            buf(1, elements), buf(1, elements), buf(1, elements), buf(1, elements),
            ints(1, elements), ints(2, points), buf(2, points), buf(1, points), ints(1, points),
            ints(1, points), buf(9, cells, phi_width), pltpu.VMEM(basis.shape[1:], jnp.bfloat16),
            buf(*tiles.shape), buf(*disp.shape),
            buf(2 * comps + 1, cols, width), buf(2 * comps + 1, cols, width),
            buf(cols, width), buf(cols, width),
            buf(STEPS, comps, cols, width), buf(STEPS, comps, cols, width),
            buf(STEPS, comps, cols, width), buf(STEPS, comps, cols, width),
            buf(n, 8, width), buf(n, comps, slot, width), buf(n // 2 + 1, 3 * cells, width),
            buf(az, 9, cells, phi_width),
            buf(az, cells, phi_width), buf(az, cells, phi_width),
            buf(2, az, layers, phi_width), buf(2, az, layers, phi_width),
            dma, dma, dma, dma, dma((2, STEPS)), dma((2, STEPS)), dma((n,)), dma((n,)),
            dma((az,)), dma((az,)), dma((n,)), dma((n,)), dma((n,)), dma((n,)),
            dma((az,)), dma((az,)), dma((2, az)), dma((2, az)), dma((15,)), dma,
        ],
        compiler_params=pltpu.CompilerParams(
            collective_id=0, has_side_effects=True, vmem_limit_bytes=40 * 1024 * 1024
        ),
    )(
        disp, vel, modulus, hoop, coupling, density, orders, element.T, local.T,
        scale.reshape(1, points), owner.T, cell.reshape(1, points),
        adjoint.reshape(9, cells, phi_width), jnp.asarray(basis), jnp.asarray(tiles),
    )
    return final, smoothed.reshape(layers, lats, phi_width)


def solution(mesh):
    field = P(None, None, "mer", "az")
    placed = (
        field, field, P(None, "mer"), P(None, "mer"), P(None, "mer"), P(None, "mer"),
        P(None, "mer"), P("mer", None), P("mer", None), P("mer"), P("mer", None), P("mer"), field,
    )
    return jax.shard_map(
        functools.partial(on_device, mesh.shape["mer"], mesh.shape["az"]),
        mesh=mesh,
        in_specs=placed,
        out_specs=(field, P(None, "mer", "az")),
        check_vma=False,
    )
```

```python
import functools
import math

import jax
import jax.numpy as jnp
import ml_dtypes
import numpy as np
from jax import lax
from jax.experimental import pallas as pl
from jax.experimental.pallas import tpu as pltpu
from jax.sharding import PartitionSpec as P

ORDERS = 256
STEPS = 3
step_scale = 0.015
smooth_rate = 0.125
MESH = pl.DeviceIdType.MESH


def gll_tables():
    nodes = np.array([-1.0, -math.sqrt(3.0 / 7.0), 0.0, math.sqrt(3.0 / 7.0), 1.0])
    weights = np.array([0.1, 49.0 / 90.0, 32.0 / 45.0, 49.0 / 90.0, 0.1])
    monomials = np.zeros((5, 5))
    for j in range(5):
        poly = np.array([1.0])
        for l in range(5):
            if l != j:
                poly = np.convolve(poly, np.array([1.0, -nodes[l]]) / (nodes[j] - nodes[l]))
        monomials[j] = poly[::-1]
    slopes = monomials[:, 1:] * np.arange(1, 5)
    derivative = np.array(
        [[sum(slopes[j, p] * nodes[i] ** p for p in range(4)) for j in range(5)] for i in range(5)]
    )
    stiffness = derivative.T @ np.diag(weights) @ derivative
    return weights, monomials, slopes, stiffness


def point_table(elements, cols, lanes):
    _, monomials, slopes, _ = gll_tables()
    both = np.concatenate([monomials, slopes], axis=1)
    table = np.zeros((1 + elements, 9, cols, lanes), np.float32)
    table[0, :, 0:5] = both.T[:, :, None]
    for e in range(elements):
        for c in range(cols):
            if 0 <= c - 4 * e <= 4:
                table[1 + e, :, c] = both[c - 4 * e][:, None]
    return table.reshape(-1, cols, lanes)


def column_table(elements, cols, lanes):
    weights, _, _, stiffness = gll_tables()
    table = np.zeros((elements, cols + 2, cols, lanes), np.float32)
    for e in range(elements):
        for c in range(cols):
            b = c - 4 * e
            if not 0 <= b <= 4:
                continue
            table[e, 0, c] = weights[b]
            for d in range(cols):
                other = (c - d) % cols - 4 * e
                if 0 <= other <= 4:
                    table[e, 1 + d, c] = stiffness[b, other]
            if cols - 4 * e == 4:
                table[e, cols + 1, c] = stiffness[b, 4]
    return table


def rim_table(cols, lanes):
    _, _, _, stiffness = gll_tables()
    table = np.zeros((cols, cols, lanes), np.float32)
    for d in range(cols):
        for a in range(5):
            other = (a - d) % cols
            if other <= 4:
                table[d, a] = stiffness[a, other]
    return table


def basis_tables(az_count, width, phi_width):
    coefs, phis = az_count * width, az_count * phi_width
    k, j = np.arange(coefs)[:, None], np.arange(phis)[None, :]
    angles = (k // 2) * j % (2 * ORDERS) * (2.0 * math.pi / (2 * ORDERS))
    basis = np.where(k % 2 == 0, np.cos(angles), np.sin(angles)) / math.sqrt(ORDERS)
    basis = basis.reshape(az_count, width, az_count, phi_width)
    turned = [
        np.concatenate([basis[q, :, (q + h) % az_count] for h in range(az_count)], axis=1)
        for q in range(az_count)
    ]
    basis = np.stack(turned).astype(np.float32)
    high = basis.astype(ml_dtypes.bfloat16)
    low = (basis - high.astype(np.float32)).astype(ml_dtypes.bfloat16)
    return np.concatenate([high, high, low], axis=1)


def halves(x):
    high = x.astype(jnp.bfloat16)
    return high, (x - high.astype(jnp.float32)).astype(jnp.bfloat16)


def dot(x, y):
    return jnp.dot(x, y, preferred_element_type=jnp.float32)


def left_parts(x):
    high, low = halves(x)
    return jnp.concatenate([high, low, high], axis=1)


def right_parts(x):
    high, low = halves(x)
    return jnp.concatenate([high, high, low], axis=0)


def kernel(
    n, az, disp_a, vel_a, modulus_a, hoop_a, coupling_a, density_a, orders_a, element_a, local_a,
    scale_a, owner_a, cell_a, adjoint_a, basis_a, tiles_a, out_u, out_k,
    disp, vel, modulus, hoop, coupling, density, orders, element, local, scale, owner, cell,
    adjoint, basis, tiles, final,
    halo_out, halo_in, dens_out, dens_in, fl_out, fr_out, fl_in, fr_in, meta, gathered, mix,
    adj_all, part_out, part_in, face_out, face_in,
    halo_s, halo_r, dens_s, dens_r, f_s, f_r, meta_s, meta_r, aa_s, aa_r, ab_s, ab_r, ga_s, ga_r, gb_s, gb_r,
    part_s, part_r, face_s, face_r, in_s, out_s,
):
    o, q = lax.axis_index("mer"), lax.axis_index("az")
    comps, nr, cols, width = disp.shape
    elements = modulus.shape[1]
    points = owner.shape[1]
    slot = gathered.shape[2]
    nodes = nr * cols
    cells = adjoint.shape[1]
    depth = face_in.shape[2]
    lats = cells // depth
    weights, _, _, stiffness = gll_tables()
    has_left, has_right = o > 0, o < n - 1
    pairs = [
        (disp_a, disp), (vel_a, vel), (modulus_a, modulus), (hoop_a, hoop), (coupling_a, coupling),
        (density_a, density), (orders_a, orders), (element_a, element), (local_a, local),
        (scale_a, scale), (owner_a, owner), (cell_a, cell), (tiles_a, tiles), (adjoint_a, adjoint),
        (basis_a.at[q], basis),
    ]
    fetches = [pltpu.make_async_copy(src, dst, in_s.at[i]) for i, (src, dst) in enumerate(pairs)]
    for fetch in fetches:
        fetch.start()

    halo_in[...] = jnp.zeros_like(halo_in)
    dens_in[...] = jnp.zeros_like(dens_in)
    fl_in[...] = jnp.zeros_like(fl_in)
    fr_in[...] = jnp.zeros_like(fr_in)
    face_in[...] = jnp.zeros_like(face_in)
    gathered[:, :, nodes:, :] = jnp.zeros((n, comps, slot - nodes, width), jnp.float32)

    barrier = pltpu.get_barrier_semaphore()

    @pl.loop(1, n)
    def _(h):
        pl.semaphore_signal(barrier, inc=1, device_id=(lax.rem(o + h, n), q), device_id_type=MESH)

    for h in range(1, az):
        r = lax.rem(q + h, az)
        pl.semaphore_signal(barrier, inc=1, device_id=(o, r), device_id_type=MESH)

        @pl.when(has_left)
        def _():
            pl.semaphore_signal(barrier, inc=1, device_id=(o - 1, r), device_id_type=MESH)

        @pl.when(has_right)
        def _():
            pl.semaphore_signal(barrier, inc=1, device_id=(o + 1, r), device_id_type=MESH)

    for fetch in fetches[:-2]:
        fetch.wait()

    row = lax.broadcasted_iota(jnp.int32, (cols, width), 0)
    lane = lax.broadcasted_iota(jnp.int32, (1, width), 1)
    u = [disp[:, a] for a in range(nr)]
    v = [vel[:, a] for a in range(nr)]

    def first_column(values):
        total = jnp.zeros((comps, cols, width), jnp.float32)
        for a in range(nr):
            total = jnp.where((row == a)[None], values[a][:, 0:1, :], total)
        return total

    halo_out[0:comps] = first_column(u)
    halo_out[comps : 2 * comps] = first_column(v)
    halo_out[2 * comps] = jnp.broadcast_to(density[0:1, 0:1], (cols, width))
    dens_out[...] = jnp.broadcast_to(
        density[0:1, elements - 1 : elements], (cols, width)
    )
    spare = jnp.zeros((1, width - points), jnp.float32) if width > points else None

    def wide(line):
        return line if spare is None else jnp.concatenate([line, spare], axis=1)

    meta[o] = jnp.concatenate(
        [
            wide(local[0:1, :]),
            wide(local[1:2, :]),
            wide((element[1:2, :] % elements).astype(jnp.float32)),
            wide(owner[...].astype(jnp.float32)),
            wide(scale[...]),
            wide(cell[...].astype(jnp.float32)),
            jnp.zeros((2, width), jnp.float32),
        ],
        axis=0,
    )

    pl.semaphore_wait(
        barrier,
        n - 1 + (az - 1) * (1 + has_left.astype(jnp.int32) + has_right.astype(jnp.int32)),
    )

    def remote(src, dst, send, recv, device):
        return pltpu.make_async_remote_copy(
            src_ref=src, dst_ref=dst, send_sem=send, recv_sem=recv,
            device_id=device, device_id_type=MESH,
        )

    to_left = lambda: remote(halo_out, halo_in, halo_s, halo_r, (o - 1, q))
    to_right = lambda: remote(dens_out, dens_in, dens_s, dens_r, (o + 1, q))
    pl.when(has_left)(lambda: to_left().start())
    pl.when(has_right)(lambda: to_right().start())

    def meta_copy(h):
        return remote(meta.at[o], meta.at[o], meta_s.at[h], meta_r.at[h], (lax.rem(o + h, n), q))

    pl.loop(1, n)(lambda h: meta_copy(h).start())

    q_lo, q_hi, q_groups = lax.rem(q, 2), lax.div(q, 2), az // 2
    q_partner = q_hi * 2 + 1 - q_lo

    def adj_far(h):
        to = lax.rem(q_hi + h, q_groups) * 2 + q_lo
        return remote(adjoint, adj_all.at[q], aa_s.at[h], aa_r.at[h], (o, to))

    def adj_near(h):
        at = lax.rem(q_hi + q_groups - h, q_groups) * 2 + q_lo
        src = adjoint if h == 0 else adj_all.at[at]
        return remote(src, adj_all.at[at], ab_s.at[h], ab_r.at[h], (o, q_partner))

    order = (q * width + lane) // 2
    ratio = order.astype(jnp.float32) / ORDERS
    even = (lane % 2 == 0)
    one = lambda ref, e: ref[0:1, e : e + 1]
    keep = [jnp.where(order < one(orders, e), 1.0, 0.0) for e in range(elements)]
    mod = [one(modulus, e) * keep[e] for e in range(elements)]
    hp = [one(hoop, e) * keep[e] * (ratio * ratio) for e in range(elements)]
    cp = [one(coupling, e) * keep[e] * ratio for e in range(elements)]
    points_at = 0
    cols_at = 9 * (1 + elements)
    rim_at = cols_at + elements * (cols + 2)
    cols_t = lambda e, which: tiles[cols_at + e * (cols + 2) + which]
    last = elements - 1
    w_end = float(weights[4])

    def blend(per_element, which):
        total = per_element[0] * cols_t(0, which)
        for e in range(1, elements):
            total = total + per_element[e] * cols_t(e, which)
        return total

    c_radial, c_hoop, c_pair = blend(mod, 0), blend(hp, 0), blend(cp, 0)
    c_colat = [blend(mod, 1 + d) for d in range(cols)]
    c_rim = mod[last] * cols_t(last, cols + 1)
    w_rim = jnp.zeros((cols, width), jnp.float32)
    for a in range(nr):
        w_rim = jnp.where(row == a, float(weights[a]), w_rim)
    r_radial = [mod[last] * w_end * tiles[rim_at + d] for d in range(cols)]
    r_radial[0] = r_radial[0] + w_rim * (
        mod[last] * float(stiffness[4, 4]) + hp[last] * w_end
    )
    r_pair = w_rim * (cp[last] * w_end)

    pl.when(has_right)(lambda: to_left().wait_recv())
    pl.when(has_left)(lambda: to_right().wait_recv())
    col_mass = one(density, 0) * cols_t(0, 0)
    for e in range(1, elements):
        col_mass = col_mass + one(density, e) * cols_t(e, 0)
    col_mass = col_mass + jnp.where(row == 0, w_end * dens_in[...], 0.0)
    rim_mass = w_end * (one(density, last) + halo_in[2 * comps])
    inv_main = [step_scale / (float(weights[a]) * col_mass) for a in range(nr)]
    inv_rim = step_scale / (jnp.where(row < nr, w_rim, 1.0) * rim_mass)
    inv_rim = jnp.where(has_right, inv_rim, 0.0)

    rim = halo_in[0:comps]
    rim_before = rim - halo_in[comps : 2 * comps]
    before = [u[a] - v[a] for a in range(nr)]

    def swap(x):
        axis = x.ndim - 1
        return jnp.where(even, pltpu.roll(x, width - 1, axis), -pltpu.roll(x, 1, axis))

    def pair(x, factor):
        return jnp.stack(
            [factor * swap(x[2]), jnp.zeros((cols, width), jnp.float32), -factor * swap(x[0])]
        )

    def left_force(step):
        return remote(fl_out.at[step], fr_in.at[step], f_s.at[0, step], f_r.at[0, step], (o - 1, q))

    def right_force(step):
        return remote(fr_out.at[step], fl_in.at[step], f_s.at[1, step], f_r.at[1, step], (o + 1, q))

    wanted = lax.broadcasted_iota(jnp.int32, (cells, width), 0).astype(jnp.float32)
    upper = lane >= slot
    blank = jnp.zeros((slot - nodes, width), jnp.float32)
    _, monomials, slopes, _ = gll_tables()

    def horner(x, coefs):
        total = coefs[-1]
        for coef in coefs[-2::-1]:
            total = total * x + coef
        return total

    def tile_horner(x, at, count):
        return horner(x, [tiles[points_at + at + p] for p in range(count)])

    def block_mix(i):
        line = lambda k: meta[i, k : k + 1, :]
        xi, eta, spot, factor = line(0), line(1), line(2), line(4)
        l_xi, s_xi = tile_horner(xi, 0, 5), tile_horner(xi, 5, 4)
        l_eta, s_eta = tile_horner(eta, 9, 5), tile_horner(eta, 14, 4)
        for e in range(1, elements):
            here = spot == float(e)
            l_eta = jnp.where(here, tile_horner(eta, 9 + 9 * e, 5), l_eta)
            s_eta = jnp.where(here, tile_horner(eta, 14 + 9 * e, 4), s_eta)
        at_end = spot == float(elements - 1)
        l_end = jnp.where(at_end, horner(eta, [float(x) for x in monomials[4]]), 0.0)
        s_end = jnp.where(at_end, horner(eta, [float(x) for x in slopes[4]]), 0.0)
        parts = []
        for x, y, y_end in (
            (s_xi, l_eta, l_end), (l_xi, s_eta, s_end), (factor * l_xi, l_eta, l_end)
        ):
            parts += [x[a : a + 1, :] * y for a in range(nr)] + [blank]
            end = x * y_end
            parts += [jnp.where(row == 0, end[a : a + 1, :], 0.0) for a in range(nr)] + [blank]
        high, low = halves(jnp.concatenate(parts, axis=0))
        chosen = (line(3) == o.astype(jnp.float32)) & (line(5) == wanted)
        chosen = chosen & (lane < points)
        chosen = jnp.where(chosen, 1.0, 0.0).astype(jnp.bfloat16)
        taken = lax.dot_general(
            jnp.concatenate([chosen, chosen], axis=1),
            jnp.concatenate([high, low], axis=1),
            (((1,), (1,)), ((), ())),
            preferred_element_type=jnp.float32,
        )
        return jnp.concatenate([taken[:, t * width : (t + 1) * width] for t in range(3)], axis=0)

    def mix_blocks(start, stop):
        @pl.loop(start, stop)
        def _(j):
            first, second = block_mix(2 * j), pltpu.roll(block_mix(2 * j + 1), slot, 1)
            mix[j] = mix[j] + first + jnp.where(upper, second, 0.0)
            mix[j + 1] = mix[j + 1] + jnp.where(upper, 0.0, second)

    for step in range(STEPS):
        forces, rim_force = [], jnp.zeros((comps, cols, width), jnp.float32)
        for a in range(nr):
            w_a = float(weights[a])
            colat = c_rim * rim[:, a : a + 1, :] + c_colat[0] * u[a]
            for d in range(1, cols):
                colat = colat + c_colat[d] * pltpu.roll(u[a], d, 1)
            radial = float(stiffness[a, 0]) * u[0]
            for i in range(1, nr):
                radial = radial + float(stiffness[a, i]) * u[i]
            force = pair(u[a], w_a * c_pair) - (
                c_radial * radial + w_a * (colat + c_hoop * u[a])
            )
            forces.append(force)
            ending = jnp.sum(c_rim * u[a], axis=1, keepdims=True)
            rim_force = jnp.where((row == a)[None], -w_a * ending, rim_force)
        rim_force = rim_force + pair(rim, r_pair)
        for d in range(cols):
            rim_force = rim_force - r_radial[d] * (pltpu.roll(rim, d, 1) if d else rim)
        fl_out[step] = first_column(forces)
        fr_out[step] = rim_force
        pl.when(has_left)(lambda: left_force(step).start())
        pl.when(has_right)(lambda: right_force(step).start())
        ahead = [2.0 * u[a] - before[a] + inv_main[a] * forces[a] for a in range(nr)]
        if step == 0:
            pl.loop(1, n)(lambda h: meta_copy(h).wait_recv())
            mix[...] = jnp.zeros_like(mix)
        if step == 0:
            fetches[-2].wait()
            for h in range(1, q_groups):
                adj_far(h).start()
            adj_near(0).start()
        if step == STEPS - 1:
            for h in range(1, q_groups):
                adj_far(h).wait_recv()
                adj_near(h).start()
        mix_blocks(n // 2 * step // STEPS, n // 2 * (step + 1) // STEPS)
        pl.when(has_right)(lambda: left_force(step).wait_recv())
        pl.when(has_left)(lambda: right_force(step).wait_recv())
        from_left = fl_in[step]
        for a in range(nr):
            ahead[a] = ahead[a] + jnp.where(
                (row == 0)[None], inv_main[a] * from_left[:, a : a + 1, :], 0.0
            )
        rim_ahead = 2.0 * rim - rim_before + inv_rim * (rim_force + fr_in[step])
        rim_ahead = jnp.where(has_right, rim_ahead, 0.0)
        before, u, rim_before, rim = u, ahead, rim, rim_ahead

    for a in range(nr):
        gathered[o, :, a * cols : (a + 1) * cols, :] = u[a]
    lo, hi, groups = lax.rem(o, 2), lax.div(o, 2), n // 2
    partner = hi * 2 + 1 - lo

    def far(h):
        block = gathered.at[o, :, 0:nodes, :]
        to = lax.rem(hi + h, groups) * 2 + lo
        return remote(block, block, ga_s.at[h], ga_r.at[h], (to, q))

    def near(h):
        block = gathered.at[lax.rem(hi + groups - h, groups) * 2 + lo, :, 0:nodes, :]
        return remote(block, block, gb_s.at[h], gb_r.at[h], (partner, q))

    pl.loop(1, groups)(lambda h: far(h).start())
    near(0).start()
    for a in range(nr):
        final[:, a] = u[a]
    final_copy = pltpu.make_async_copy(final, out_u, out_s)
    final_copy.start()

    def add_group(h, total):
        near(h).wait_recv()
        j = lax.rem(hi + groups - h, groups)
        block = [
            jnp.concatenate([gathered[2 * j, s], gathered[2 * j + 1, s]], axis=0)
            for s in range(comps)
        ]
        return total + dot(left_parts(mix[j]), right_parts(jnp.concatenate(block, axis=1)))

    def next_group(h, total):
        far(h).wait_recv()
        near(h).start()
        return add_group(h - 1, total)

    coefs = lax.fori_loop(
        1, groups, next_group, jnp.zeros((3 * cells, comps * width), jnp.float32)
    )
    coefs = add_group(groups - 1, coefs)
    fetches[-1].wait()
    for h in range(q_groups):
        adj_near(h).wait_recv()
    coefs = [coefs[:, s * width : (s + 1) * width] for s in range(comps)]
    rows = []
    for s in range(comps):
        rows.append(coefs[s][0 : 2 * cells])
        rows.append(swap(coefs[s][2 * cells :]) * ratio)
    samples = dot(left_parts(jnp.concatenate(rows, axis=0)), basis[...])
    raw = []
    for h in range(az):
        total = jnp.zeros((cells, width), jnp.float32)
        for g in range(3 * comps):
            values = adjoint[g] if h == 0 else adj_all[lax.rem(q + h, az), g]
            at = samples[g * cells : (g + 1) * cells, h * width : (h + 1) * width]
            total = total + at * values
        raw.append(total)
    raw = jnp.concatenate(raw, axis=1)
    whole = az * width
    tile_lat = lax.broadcasted_iota(jnp.int32, (depth, width), 0) % lats
    for h in range(az):
        low_face = jnp.zeros((depth, width), jnp.float32)
        high_face = jnp.zeros((depth, width), jnp.float32)
        for i in range(cells // depth):
            tile = raw[i * depth : (i + 1) * depth, h * width : (h + 1) * width]
            first = pltpu.roll(jnp.where(tile_lat == 0, tile, 0.0), i, 0) if i else (
                jnp.where(tile_lat == 0, tile, 0.0)
            )
            low_face = low_face + first
            turn = (i + depth - (lats - 1)) % depth
            final_row = jnp.where(tile_lat == lats - 1, tile, 0.0)
            high_face = high_face + (pltpu.roll(final_row, turn, 0) if turn else final_row)
        face_out[0, h] = low_face
        face_out[1, h] = high_face

    def face_left(h):
        return remote(
            face_out.at[0, h], face_in.at[1, h], face_s.at[0, h], face_r.at[0, h],
            (o - 1, lax.rem(q + h, az)),
        )

    def face_right(h):
        return remote(
            face_out.at[1, h], face_in.at[0, h], face_s.at[1, h], face_r.at[1, h],
            (o + 1, lax.rem(q + h, az)),
        )

    for h in range(az):
        pl.when(has_left)(lambda: face_left(h).start())
        pl.when(has_right)(lambda: face_right(h).start())
    level = lax.broadcasted_iota(jnp.int32, (cells, whole), 0)
    lat = level % lats
    around = pltpu.roll(raw, 1, 1) + pltpu.roll(raw, whole - 1, 1)
    around = around + jnp.where(lat > 0, pltpu.roll(raw, 1, 0), 0.0)
    around = around + jnp.where(lat < lats - 1, pltpu.roll(raw, cells - 1, 0), 0.0)
    around = around + jnp.where(level >= lats, pltpu.roll(raw, lats, 0), 0.0)
    around = around + jnp.where(level < cells - lats, pltpu.roll(raw, cells - lats, 0), 0.0)
    smooth = (1.0 - 6.0 * smooth_rate) * raw + smooth_rate * around

    def part_copy(h):
        return remote(
            part_out.at[h], part_in.at[h], part_s.at[h], part_r.at[h], (o, lax.rem(q + h, az))
        )

    for h in range(1, az):
        part_out[h] = smooth[:, h * width : (h + 1) * width]
        part_copy(h).start()
    result = smooth[:, 0:width]
    for h in range(1, az):
        part_copy(h).wait_recv()
        result = result + part_in[h]
    for h in range(az):
        pl.when(has_right)(lambda: face_left(h).wait_recv())
        pl.when(has_left)(lambda: face_right(h).wait_recv())
    below, above = face_in[0, 0], face_in[1, 0]
    for h in range(1, az):
        below, above = below + face_in[0, h], above + face_in[1, h]
    for i in range(cells // depth):
        turn = (lats - 1 - i) % depth
        first = pltpu.roll(below, (depth - i) % depth, 0) if i else below
        final_row = pltpu.roll(above, turn, 0) if turn else above
        extra = jnp.where(tile_lat == 0, first, 0.0) + jnp.where(
            tile_lat == lats - 1, final_row, 0.0
        )
        at = slice(i * depth, (i + 1) * depth)
        out_k[at] = result[at] + smooth_rate * extra

    final_copy.wait()
    pl.when(has_left)(lambda: to_left().wait_send())
    pl.when(has_right)(lambda: to_right().wait_send())
    pl.loop(1, n)(lambda h: meta_copy(h).wait_send())
    for step in range(STEPS):
        pl.when(has_left)(lambda: left_force(step).wait_send())
        pl.when(has_right)(lambda: right_force(step).wait_send())
    for h in range(q_groups):
        adj_near(h).wait_send()
        if h:
            adj_far(h).wait_send()
    for h in range(1, az):
        part_copy(h).wait_send()
    for h in range(az):
        pl.when(has_left)(lambda: face_left(h).wait_send())
        pl.when(has_right)(lambda: face_right(h).wait_send())
    pl.loop(1, groups)(lambda h: far(h).wait_send())
    pl.loop(0, groups)(lambda h: near(h).wait_send())


def on_device(
    n, az, disp, vel, modulus, hoop, coupling, density, orders, element, local, scale, owner, cell,
    adjoint,
):
    comps, nr, cols, width = disp.shape
    elements, points = modulus.shape[1], owner.shape[0]
    layers, lats, phi_width = adjoint.shape[1:]
    cells = layers * lats
    assert nr == 5 and cols == 4 * elements and layers == 8 and layers % lats == 0
    assert points <= width and width == phi_width
    tiles = np.concatenate(
        [
            point_table(elements, cols, width),
            column_table(elements, cols, width).reshape(-1, cols, width),
            rim_table(cols, width),
        ]
    )
    basis = basis_tables(az, width, phi_width)
    vm = pl.BlockSpec(memory_space=pltpu.VMEM)
    anywhere = pl.BlockSpec(memory_space=pltpu.HBM)
    slot = width // 2
    f32, dma = jnp.float32, pltpu.SemaphoreType.DMA
    buf = lambda *shape: pltpu.VMEM(shape, f32)
    ints = lambda *shape: pltpu.VMEM(shape, jnp.int32)
    final, smoothed = pl.pallas_call(
        functools.partial(kernel, n, az),
        out_shape=(
            jax.ShapeDtypeStruct(disp.shape, f32),
            jax.ShapeDtypeStruct((cells, phi_width), f32),
        ),
        in_specs=[anywhere] * 15,
        out_specs=(anywhere, vm),
        scratch_shapes=[
            buf(*disp.shape), buf(*vel.shape),
            buf(1, elements), buf(1, elements), buf(1, elements), buf(1, elements),
            ints(1, elements), ints(2, points), buf(2, points), buf(1, points), ints(1, points),
            ints(1, points), buf(9, cells, phi_width), pltpu.VMEM(basis.shape[1:], jnp.bfloat16),
            buf(*tiles.shape), buf(*disp.shape),
            buf(2 * comps + 1, cols, width), buf(2 * comps + 1, cols, width),
            buf(cols, width), buf(cols, width),
            buf(STEPS, comps, cols, width), buf(STEPS, comps, cols, width),
            buf(STEPS, comps, cols, width), buf(STEPS, comps, cols, width),
            buf(n, 8, width), buf(n, comps, slot, width), buf(n // 2 + 1, 3 * cells, width),
            buf(az, 9, cells, phi_width),
            buf(az, cells, phi_width), buf(az, cells, phi_width),
            buf(2, az, layers, phi_width), buf(2, az, layers, phi_width),
            dma, dma, dma, dma, dma((2, STEPS)), dma((2, STEPS)), dma((n,)), dma((n,)),
            dma((az,)), dma((az,)), dma((az,)), dma((az,)),
            dma((n,)), dma((n,)), dma((n,)), dma((n,)),
            dma((az,)), dma((az,)), dma((2, az)), dma((2, az)), dma((15,)), dma,
        ],
        compiler_params=pltpu.CompilerParams(
            collective_id=0, has_side_effects=True, vmem_limit_bytes=60 * 1024 * 1024
        ),
    )(
        disp, vel, modulus, hoop, coupling, density, orders, element.T, local.T,
        scale.reshape(1, points), owner.T, cell.reshape(1, points),
        adjoint.reshape(9, cells, phi_width), jnp.asarray(basis), jnp.asarray(tiles),
    )
    return final, smoothed.reshape(layers, lats, phi_width)


def solution(mesh):
    field = P(None, None, "mer", "az")
    placed = (
        field, field, P(None, "mer"), P(None, "mer"), P(None, "mer"), P(None, "mer"),
        P(None, "mer"), P("mer", None), P("mer", None), P("mer"), P("mer", None), P("mer"), field,
    )
    return jax.shard_map(
        functools.partial(on_device, mesh.shape["mer"], mesh.shape["az"]),
        mesh=mesh,
        in_specs=placed,
        out_specs=(field, P(None, "mer", "az")),
        check_vma=False,
    )
```

```python
import functools
import math

import jax
import jax.numpy as jnp
import ml_dtypes
import numpy as np
from jax import lax
from jax.experimental import pallas as pl
from jax.experimental.pallas import tpu as pltpu
from jax.sharding import PartitionSpec as P

ORDERS = 256
STEPS = 3
step_scale = 0.015
smooth_rate = 0.125
MESH = pl.DeviceIdType.MESH


def gll_tables():
    nodes = np.array([-1.0, -math.sqrt(3.0 / 7.0), 0.0, math.sqrt(3.0 / 7.0), 1.0])
    weights = np.array([0.1, 49.0 / 90.0, 32.0 / 45.0, 49.0 / 90.0, 0.1])
    monomials = np.zeros((5, 5))
    for j in range(5):
        poly = np.array([1.0])
        for l in range(5):
            if l != j:
                poly = np.convolve(poly, np.array([1.0, -nodes[l]]) / (nodes[j] - nodes[l]))
        monomials[j] = poly[::-1]
    slopes = monomials[:, 1:] * np.arange(1, 5)
    derivative = np.array(
        [[sum(slopes[j, p] * nodes[i] ** p for p in range(4)) for j in range(5)] for i in range(5)]
    )
    stiffness = derivative.T @ np.diag(weights) @ derivative
    return weights, monomials, slopes, stiffness


def point_table(elements, cols, lanes):
    _, monomials, slopes, _ = gll_tables()
    both = np.concatenate([monomials, slopes], axis=1)
    table = np.zeros((1 + elements, 9, cols, lanes), np.float32)
    table[0, :, 0:5] = both.T[:, :, None]
    for e in range(elements):
        for c in range(cols):
            if 0 <= c - 4 * e <= 4:
                table[1 + e, :, c] = both[c - 4 * e][:, None]
    return table.reshape(-1, cols, lanes)


def column_table(elements, cols, lanes):
    weights, _, _, stiffness = gll_tables()
    table = np.zeros((elements, cols + 2, cols, lanes), np.float32)
    for e in range(elements):
        for c in range(cols):
            b = c - 4 * e
            if not 0 <= b <= 4:
                continue
            table[e, 0, c] = weights[b]
            for d in range(cols):
                other = (c - d) % cols - 4 * e
                if 0 <= other <= 4:
                    table[e, 1 + d, c] = stiffness[b, other]
            if cols - 4 * e == 4:
                table[e, cols + 1, c] = stiffness[b, 4]
    return table


def rim_table(cols, lanes):
    _, _, _, stiffness = gll_tables()
    table = np.zeros((cols, cols, lanes), np.float32)
    for d in range(cols):
        for a in range(5):
            other = (a - d) % cols
            if other <= 4:
                table[d, a] = stiffness[a, other]
    return table


def basis_tables(az_count, width, phi_width):
    coefs, phis = az_count * width, az_count * phi_width
    k, j = np.arange(coefs)[:, None], np.arange(phis)[None, :]
    angles = (k // 2) * j % (2 * ORDERS) * (2.0 * math.pi / (2 * ORDERS))
    basis = np.where(k % 2 == 0, np.cos(angles), np.sin(angles)) / math.sqrt(ORDERS)
    basis = basis.reshape(az_count, width, az_count, phi_width)
    turned = [
        np.concatenate([basis[q, :, (q + h) % az_count] for h in range(az_count)], axis=1)
        for q in range(az_count)
    ]
    basis = np.stack(turned).astype(np.float32)
    high = basis.astype(ml_dtypes.bfloat16)
    low = (basis - high.astype(np.float32)).astype(ml_dtypes.bfloat16)
    return np.concatenate([high, high, low], axis=1)


def halves(x):
    high = x.astype(jnp.bfloat16)
    return high, (x - high.astype(jnp.float32)).astype(jnp.bfloat16)


def dot(x, y):
    return jnp.dot(x, y, preferred_element_type=jnp.float32)


def left_parts(x):
    high, low = halves(x)
    return jnp.concatenate([high, low, high], axis=1)


def right_parts(x):
    high, low = halves(x)
    return jnp.concatenate([high, high, low], axis=0)


def kernel(
    n, az, disp_a, vel_a, modulus_a, hoop_a, coupling_a, density_a, orders_a, element_a, local_a,
    scale_a, owner_a, cell_a, adjoint_a, basis_a, tiles_a, out_u, out_k,
    modulus, hoop, coupling, density, orders, element, local, scale, owner, cell,
    adjoint, basis, tiles,
    halo_out, halo_in, edge_out, edge_in, force_out, force_in, meta, gathered, mix,
    adj_all, part_out, part_in, face_out, face_in,
    halo_s, halo_r, edge_s, edge_r, f_s, f_r, meta_s, meta_r, aa_s, aa_r, ab_s, ab_r, ga_s, ga_r, gb_s, gb_r,
    part_s, part_r, face_s, face_r, in_s,
):
    o, q = lax.axis_index("mer"), lax.axis_index("az")
    comps, nr, cols, width = out_u.shape
    fields = comps * nr
    elements = modulus.shape[1]
    points = owner.shape[1]
    slot = gathered.shape[2]
    nodes = nr * cols
    cells = adjoint.shape[1]
    depth = face_in.shape[2]
    lats = cells // depth
    weights, _, _, stiffness = gll_tables()
    has_left, has_right = o > 0, o < n - 1
    has_left_2, has_right_2 = o > 1, o < n - 2
    pairs = [
        (disp_a, halo_out.at[0:fields]), (vel_a, halo_out.at[fields : 2 * fields]), (modulus_a, modulus), (hoop_a, hoop), (coupling_a, coupling),
        (density_a, density), (orders_a, orders), (element_a, element), (local_a, local),
        (scale_a, scale), (owner_a, owner), (cell_a, cell), (tiles_a, tiles), (adjoint_a, adjoint),
        (basis_a.at[q], basis),
    ]
    fetches = [pltpu.make_async_copy(src, dst, in_s.at[i]) for i, (src, dst) in enumerate(pairs)]
    for fetch in fetches:
        fetch.start()

    halo_in[...] = jnp.zeros_like(halo_in)
    edge_in[...] = jnp.zeros_like(edge_in)
    force_in[...] = jnp.zeros_like(force_in)
    face_in[...] = jnp.zeros_like(face_in)
    gathered[:, :, nodes:, :] = jnp.zeros((n, comps, slot - nodes, width), jnp.float32)

    barrier = pltpu.get_barrier_semaphore()

    @pl.loop(1, n)
    def _(h):
        pl.semaphore_signal(barrier, inc=1, device_id=(lax.rem(o + h, n), q), device_id_type=MESH)

    for h in range(1, az):
        r = lax.rem(q + h, az)
        pl.semaphore_signal(barrier, inc=1, device_id=(o, r), device_id_type=MESH)

        @pl.when(has_left)
        def _():
            pl.semaphore_signal(barrier, inc=1, device_id=(o - 1, r), device_id_type=MESH)

        @pl.when(has_right)
        def _():
            pl.semaphore_signal(barrier, inc=1, device_id=(o + 1, r), device_id_type=MESH)

    for fetch in fetches[:-2]:
        fetch.wait()

    row = lax.broadcasted_iota(jnp.int32, (cols, width), 0)
    lane = lax.broadcasted_iota(jnp.int32, (1, width), 1)

    def field(ref, kind):
        at = lambda s, a: ref[kind * fields + s * nr + a]
        return [jnp.stack([at(s, a) for s in range(comps)]) for a in range(nr)]

    u, v = field(halo_out, 0), field(halo_out, 1)

    def first_column(values):
        total = jnp.zeros((comps, cols, width), jnp.float32)
        for a in range(nr):
            total = jnp.where((row == a)[None], values[a][:, 0:1, :], total)
        return total

    edge_out[0:comps] = first_column(u)
    edge_out[comps:] = first_column(v)
    one = lambda ref, e: ref[0:1, e : e + 1].astype(jnp.float32)
    known = jnp.zeros((2 * cols, width), jnp.float32)
    row_2 = lax.broadcasted_iota(jnp.int32, (2 * cols, width), 0)
    for i, ref in enumerate((modulus, hoop, coupling, density, orders)):
        for e in range(elements):
            known = jnp.where(row_2 == 5 * e + i, one(ref, e), known)
    halo_out[2 * fields] = known[0:cols]
    halo_out[2 * fields + 1] = known[cols:]
    spare = jnp.zeros((1, width - points), jnp.float32) if width > points else None

    def wide(line):
        return line if spare is None else jnp.concatenate([line, spare], axis=1)

    meta[o] = jnp.concatenate(
        [
            wide(local[0:1, :]),
            wide(local[1:2, :]),
            wide((element[1:2, :] % elements).astype(jnp.float32)),
            wide(owner[...].astype(jnp.float32)),
            wide(scale[...]),
            wide(cell[...].astype(jnp.float32)),
            jnp.zeros((2, width), jnp.float32),
        ],
        axis=0,
    )

    pl.semaphore_wait(
        barrier,
        n - 1 + (az - 1) * (1 + has_left.astype(jnp.int32) + has_right.astype(jnp.int32)),
    )

    def remote(src, dst, send, recv, device):
        return pltpu.make_async_remote_copy(
            src_ref=src, dst_ref=dst, send_sem=send, recv_sem=recv,
            device_id=device, device_id_type=MESH,
        )

    def to_left():
        return remote(halo_out, halo_in.at[1], halo_s.at[0], halo_r.at[0], (o - 1, q))

    def to_right():
        return remote(halo_out, halo_in.at[0], halo_s.at[1], halo_r.at[1], (o + 1, q))

    def to_left_2():
        return remote(edge_out, edge_in, edge_s, edge_r, (o - 2, q))

    def meta_copy(h):
        return remote(meta.at[o], meta.at[o], meta_s.at[h], meta_r.at[h], (lax.rem(o + h, n), q))

    pl.loop(1, n)(lambda h: meta_copy(h).start())
    pl.when(has_left)(lambda: to_left().start())
    pl.when(has_right)(lambda: to_right().start())
    pl.when(has_left_2)(lambda: to_left_2().start())

    q_lo, q_hi, q_groups = lax.rem(q, 2), lax.div(q, 2), az // 2
    q_partner = q_hi * 2 + 1 - q_lo

    def adj_far(h):
        to = lax.rem(q_hi + h, q_groups) * 2 + q_lo
        return remote(adjoint, adj_all.at[q], aa_s.at[h], aa_r.at[h], (o, to))

    def adj_near(h):
        at = lax.rem(q_hi + q_groups - h, q_groups) * 2 + q_lo
        src = adjoint if h == 0 else adj_all.at[at]
        return remote(src, adj_all.at[at], ab_s.at[h], ab_r.at[h], (o, q_partner))

    fetches[-2].wait()
    for h in range(1, q_groups):
        adj_far(h).start()
    adj_near(0).start()

    order = (q * width + lane) // 2
    ratio = order.astype(jnp.float32) / ORDERS
    even = (lane % 2 == 0)
    last = elements - 1
    w_end = float(weights[4])
    points_at = 0
    cols_at = 9 * (1 + elements)
    rim_at = cols_at + elements * (cols + 2)
    cols_t = lambda e, which: tiles[cols_at + e * (cols + 2) + which]
    w_rim = jnp.zeros((cols, width), jnp.float32)
    for a in range(nr):
        w_rim = jnp.where(row == a, float(weights[a]), w_rim)

    def setup(ref, before, there):
        def value(i, e):
            at = 5 * e + i
            return ref[2 * fields + at // cols, at % cols : at % cols + 1, :]

        def blend(per_element, which):
            total = per_element[0] * cols_t(0, which)
            for e in range(1, elements):
                total = total + per_element[e] * cols_t(e, which)
            return total

        keep = [jnp.where(order.astype(jnp.float32) < value(4, e), 1.0, 0.0) for e in range(elements)]
        mod = [value(0, e) * keep[e] for e in range(elements)]
        hp = [value(1, e) * keep[e] * (ratio * ratio) for e in range(elements)]
        cp = [value(2, e) * keep[e] * ratio for e in range(elements)]
        c_radial, c_hoop, c_pair = blend(mod, 0), blend(hp, 0), blend(cp, 0)
        c_colat = [blend(mod, 1 + d) for d in range(cols)]
        c_rim = mod[last] * cols_t(last, cols + 1)
        r_radial = [mod[last] * w_end * tiles[rim_at + d] for d in range(cols)]
        r_radial[0] = r_radial[0] + w_rim * (
            mod[last] * float(stiffness[4, 4]) + hp[last] * w_end
        )
        r_pair = w_rim * (cp[last] * w_end)
        mass = blend([value(3, e) for e in range(elements)], 0)
        if before is not None:
            at = 5 * last + 3
            shared = before[2 * fields + at // cols, at % cols : at % cols + 1, :]
            mass = mass + jnp.where(row == 0, w_end * shared, 0.0)
        inverse = [step_scale / (float(weights[a]) * mass) for a in range(nr)]
        if there is not None:
            inverse = [jnp.where(there, x, 0.0) for x in inverse]
        return (c_radial, c_hoop, c_pair, c_colat, c_rim, r_radial, r_pair), inverse

    def swap(x):
        axis = x.ndim - 1
        return jnp.where(even, pltpu.roll(x, width - 1, axis), -pltpu.roll(x, 1, axis))

    def pair(x, factor):
        return jnp.stack(
            [factor * swap(x[2]), jnp.zeros((cols, width), jnp.float32), -factor * swap(x[0])]
        )

    def force_copy():
        return remote(force_out, force_in, f_s, f_r, (o + 1, q))

    def main_force(u, rim, coefs):
        c_radial, c_hoop, c_pair, c_colat, c_rim, _, _ = coefs
        forces = []
        for a in range(nr):
            w_a = float(weights[a])
            colat = c_rim * rim[:, a : a + 1, :] + c_colat[0] * u[a]
            for d in range(1, cols):
                colat = colat + c_colat[d] * pltpu.roll(u[a], d, 1)
            radial = float(stiffness[a, 0]) * u[0]
            for i in range(1, nr):
                radial = radial + float(stiffness[a, i]) * u[i]
            force = pair(u[a], w_a * c_pair) - (
                c_radial * radial + w_a * (colat + c_hoop * u[a])
            )
            forces.append(force)
        return forces

    def end_force(u, rim, coefs):
        c_rim, r_radial, r_pair = coefs[4:]
        force = jnp.zeros((comps, cols, width), jnp.float32)
        for a in range(nr):
            ending = jnp.sum(c_rim * u[a], axis=1, keepdims=True)
            force = jnp.where((row == a)[None], -float(weights[a]) * ending, force)
        force = force + pair(rim, r_pair)
        for d in range(cols):
            force = force - r_radial[d] * (pltpu.roll(rim, d, 1) if d else rim)
        return force

    def with_edge(forces, edge):
        return [
            forces[a] + jnp.where((row == 0)[None], edge[:, a : a + 1, :], 0.0) for a in range(nr)
        ]

    def advance(u, before, forces, inverse):
        return [2.0 * u[a] - before[a] + inverse[a] * forces[a] for a in range(nr)]

    wanted = lax.broadcasted_iota(jnp.int32, (cells, width), 0).astype(jnp.float32)
    upper = lane >= slot
    blank = jnp.zeros((slot - nodes, width), jnp.float32)
    _, monomials, slopes, _ = gll_tables()

    def horner(x, coefs):
        total = coefs[-1]
        for coef in coefs[-2::-1]:
            total = total * x + coef
        return total

    def tile_horner(x, at, count):
        return horner(x, [tiles[points_at + at + p] for p in range(count)])

    def block_mix(i):
        line = lambda k: meta[i, k : k + 1, :]
        xi, eta, spot, factor = line(0), line(1), line(2), line(4)
        l_xi, s_xi = tile_horner(xi, 0, 5), tile_horner(xi, 5, 4)
        l_eta, s_eta = tile_horner(eta, 9, 5), tile_horner(eta, 14, 4)
        for e in range(1, elements):
            here = spot == float(e)
            l_eta = jnp.where(here, tile_horner(eta, 9 + 9 * e, 5), l_eta)
            s_eta = jnp.where(here, tile_horner(eta, 14 + 9 * e, 4), s_eta)
        at_end = spot == float(elements - 1)
        l_end = jnp.where(at_end, horner(eta, [float(x) for x in monomials[4]]), 0.0)
        s_end = jnp.where(at_end, horner(eta, [float(x) for x in slopes[4]]), 0.0)
        parts = []
        for x, y, y_end in (
            (s_xi, l_eta, l_end), (l_xi, s_eta, s_end), (factor * l_xi, l_eta, l_end)
        ):
            parts += [x[a : a + 1, :] * y for a in range(nr)] + [blank]
            end = x * y_end
            parts += [jnp.where(row == 0, end[a : a + 1, :], 0.0) for a in range(nr)] + [blank]
        high, low = halves(jnp.concatenate(parts, axis=0))
        chosen = (line(3) == o.astype(jnp.float32)) & (line(5) == wanted)
        chosen = chosen & (lane < points)
        chosen = jnp.where(chosen, 1.0, 0.0).astype(jnp.bfloat16)
        taken = lax.dot_general(
            jnp.concatenate([chosen, chosen], axis=1),
            jnp.concatenate([high, low], axis=1),
            (((1,), (1,)), ((), ())),
            preferred_element_type=jnp.float32,
        )
        return jnp.concatenate([taken[:, t * width : (t + 1) * width] for t in range(3)], axis=0)

    def mix_blocks(start, stop):
        @pl.loop(start, stop)
        def _(j):
            first, second = block_mix(2 * j), pltpu.roll(block_mix(2 * j + 1), slot, 1)
            mix[j] = mix[j] + first + jnp.where(upper, second, 0.0)
            mix[j + 1] = mix[j + 1] + jnp.where(upper, 0.0, second)

    pl.loop(1, n)(lambda h: meta_copy(h).wait_recv())
    mix[...] = jnp.zeros_like(mix)
    mix_blocks(0, n // 2)

    pl.when(has_right)(lambda: to_left().wait_recv())
    pl.when(has_left)(lambda: to_right().wait_recv())
    pl.when(has_right_2)(lambda: to_left_2().wait_recv())
    left, right = halo_in.at[0], halo_in.at[1]
    coefs_l, inverse_l = setup(left, None, has_left)
    coefs_m, inverse_m = setup(halo_out, left, None)
    coefs_r, inverse_r = setup(right, halo_out, has_right)
    u_l, u_r = field(left, 0), field(right, 0)
    before_l = [x - y for x, y in zip(u_l, field(left, 1))]
    before = [x - y for x, y in zip(u, v)]
    before_r = [x - y for x, y in zip(u_r, field(right, 1))]
    far_rim = edge_in[0:comps]

    rim_l, rim = first_column(u), first_column(u_r)
    force_l = main_force(u_l, rim_l, coefs_l)
    force_m = with_edge(main_force(u, rim, coefs_m), end_force(u_l, rim_l, coefs_l))
    force_r = with_edge(main_force(u_r, far_rim, coefs_r), end_force(u, rim, coefs_m))
    u_l = advance(u_l, before_l, force_l, inverse_l)
    before, u = u, advance(u, before, force_m, inverse_m)
    before_r, u_r = u_r, advance(u_r, before_r, force_r, inverse_r)

    rim_l, rim = first_column(u), first_column(u_r)
    force_m = with_edge(main_force(u, rim, coefs_m), end_force(u_l, rim_l, coefs_l))
    force_r = with_edge(main_force(u_r, far_rim, coefs_r), end_force(u, rim, coefs_m))
    before, u = u, advance(u, before, force_m, inverse_m)
    u_r = advance(u_r, before_r, force_r, inverse_r)

    rim = first_column(u_r)
    force_out[...] = end_force(u, rim, coefs_m)
    pl.when(has_right)(lambda: force_copy().start())
    force_m = main_force(u, rim, coefs_m)
    for h in range(1, q_groups):
        adj_far(h).wait_recv()
        adj_near(h).start()
    pl.when(has_left)(lambda: force_copy().wait_recv())
    u = advance(u, before, with_edge(force_m, force_in[...]), inverse_m)

    for a in range(nr):
        gathered[o, :, a * cols : (a + 1) * cols, :] = u[a]
    lo, hi, groups = lax.rem(o, 2), lax.div(o, 2), n // 2
    partner = hi * 2 + 1 - lo

    def far(h):
        block = gathered.at[o, :, 0:nodes, :]
        to = lax.rem(hi + h, groups) * 2 + lo
        return remote(block, block, ga_s.at[h], ga_r.at[h], (to, q))

    def near(h):
        block = gathered.at[lax.rem(hi + groups - h, groups) * 2 + lo, :, 0:nodes, :]
        return remote(block, block, gb_s.at[h], gb_r.at[h], (partner, q))

    pl.loop(1, groups)(lambda h: far(h).start())
    near(0).start()
    for a in range(nr):
        out_u[:, a] = u[a]

    def add_group(h, total):
        near(h).wait_recv()
        j = lax.rem(hi + groups - h, groups)
        block = [
            jnp.concatenate([gathered[2 * j, s], gathered[2 * j + 1, s]], axis=0)
            for s in range(comps)
        ]
        return total + dot(left_parts(mix[j]), right_parts(jnp.concatenate(block, axis=1)))

    def next_group(h, total):
        far(h).wait_recv()
        near(h).start()
        return add_group(h - 1, total)

    coefs = lax.fori_loop(
        1, groups, next_group, jnp.zeros((3 * cells, comps * width), jnp.float32)
    )
    coefs = add_group(groups - 1, coefs)
    fetches[-1].wait()
    for h in range(q_groups):
        adj_near(h).wait_recv()
    coefs = [coefs[:, s * width : (s + 1) * width] for s in range(comps)]
    rows = []
    for s in range(comps):
        rows.append(coefs[s][0 : 2 * cells])
        rows.append(swap(coefs[s][2 * cells :]) * ratio)
    samples = dot(left_parts(jnp.concatenate(rows, axis=0)), basis[...])
    raw = []
    for h in range(az):
        total = jnp.zeros((cells, width), jnp.float32)
        for g in range(3 * comps):
            values = adjoint[g] if h == 0 else adj_all[lax.rem(q + h, az), g]
            at = samples[g * cells : (g + 1) * cells, h * width : (h + 1) * width]
            total = total + at * values
        raw.append(total)
    raw = jnp.concatenate(raw, axis=1)
    whole = az * width
    tile_lat = lax.broadcasted_iota(jnp.int32, (depth, width), 0) % lats
    for h in range(az):
        low_face = jnp.zeros((depth, width), jnp.float32)
        high_face = jnp.zeros((depth, width), jnp.float32)
        for i in range(cells // depth):
            tile = raw[i * depth : (i + 1) * depth, h * width : (h + 1) * width]
            first = pltpu.roll(jnp.where(tile_lat == 0, tile, 0.0), i, 0) if i else (
                jnp.where(tile_lat == 0, tile, 0.0)
            )
            low_face = low_face + first
            turn = (i + depth - (lats - 1)) % depth
            final_row = jnp.where(tile_lat == lats - 1, tile, 0.0)
            high_face = high_face + (pltpu.roll(final_row, turn, 0) if turn else final_row)
        face_out[0, h] = low_face
        face_out[1, h] = high_face

    def face_left(h):
        return remote(
            face_out.at[0, h], face_in.at[1, h], face_s.at[0, h], face_r.at[0, h],
            (o - 1, lax.rem(q + h, az)),
        )

    def face_right(h):
        return remote(
            face_out.at[1, h], face_in.at[0, h], face_s.at[1, h], face_r.at[1, h],
            (o + 1, lax.rem(q + h, az)),
        )

    for h in range(az):
        pl.when(has_left)(lambda: face_left(h).start())
        pl.when(has_right)(lambda: face_right(h).start())
    level = lax.broadcasted_iota(jnp.int32, (cells, whole), 0)
    lat = level % lats
    around = pltpu.roll(raw, 1, 1) + pltpu.roll(raw, whole - 1, 1)
    around = around + jnp.where(lat > 0, pltpu.roll(raw, 1, 0), 0.0)
    around = around + jnp.where(lat < lats - 1, pltpu.roll(raw, cells - 1, 0), 0.0)
    around = around + jnp.where(level >= lats, pltpu.roll(raw, lats, 0), 0.0)
    around = around + jnp.where(level < cells - lats, pltpu.roll(raw, cells - lats, 0), 0.0)
    smooth = (1.0 - 6.0 * smooth_rate) * raw + smooth_rate * around

    def part_copy(h):
        return remote(
            part_out.at[h], part_in.at[h], part_s.at[h], part_r.at[h], (o, lax.rem(q + h, az))
        )

    for h in range(1, az):
        part_out[h] = smooth[:, h * width : (h + 1) * width]
        part_copy(h).start()
    result = smooth[:, 0:width]
    for h in range(1, az):
        part_copy(h).wait_recv()
        result = result + part_in[h]
    for h in range(az):
        pl.when(has_right)(lambda: face_left(h).wait_recv())
        pl.when(has_left)(lambda: face_right(h).wait_recv())
    below, above = face_in[0, 0], face_in[1, 0]
    for h in range(1, az):
        below, above = below + face_in[0, h], above + face_in[1, h]
    for i in range(cells // depth):
        turn = (lats - 1 - i) % depth
        first = pltpu.roll(below, (depth - i) % depth, 0) if i else below
        final_row = pltpu.roll(above, turn, 0) if turn else above
        extra = jnp.where(tile_lat == 0, first, 0.0) + jnp.where(
            tile_lat == lats - 1, final_row, 0.0
        )
        at = slice(i * depth, (i + 1) * depth)
        out_k[at] = result[at] + smooth_rate * extra

    pl.when(has_left)(lambda: to_left().wait_send())
    pl.when(has_right)(lambda: to_right().wait_send())
    pl.loop(1, n)(lambda h: meta_copy(h).wait_send())
    pl.when(has_left_2)(lambda: to_left_2().wait_send())
    pl.when(has_right)(lambda: force_copy().wait_send())
    for h in range(q_groups):
        adj_near(h).wait_send()
        if h:
            adj_far(h).wait_send()
    for h in range(1, az):
        part_copy(h).wait_send()
    for h in range(az):
        pl.when(has_left)(lambda: face_left(h).wait_send())
        pl.when(has_right)(lambda: face_right(h).wait_send())
    pl.loop(1, groups)(lambda h: far(h).wait_send())
    pl.loop(0, groups)(lambda h: near(h).wait_send())


def on_device(
    n, az, disp, vel, modulus, hoop, coupling, density, orders, element, local, scale, owner, cell,
    adjoint,
):
    comps, nr, cols, width = disp.shape
    elements, points = modulus.shape[1], owner.shape[0]
    layers, lats, phi_width = adjoint.shape[1:]
    cells = layers * lats
    assert STEPS == 3 and elements == 2
    assert nr == 5 and cols == 4 * elements and layers == 8 and layers % lats == 0
    assert points <= width and width == phi_width
    tiles = np.concatenate(
        [
            point_table(elements, cols, width),
            column_table(elements, cols, width).reshape(-1, cols, width),
            rim_table(cols, width),
        ]
    )
    basis = basis_tables(az, width, phi_width)
    vm = pl.BlockSpec(memory_space=pltpu.VMEM)
    anywhere = pl.BlockSpec(memory_space=pltpu.HBM)
    slot = width // 2
    f32, dma = jnp.float32, pltpu.SemaphoreType.DMA
    buf = lambda *shape: pltpu.VMEM(shape, f32)
    ints = lambda *shape: pltpu.VMEM(shape, jnp.int32)
    final, smoothed = pl.pallas_call(
        functools.partial(kernel, n, az),
        out_shape=(
            pltpu.VMEM(disp.shape, f32),
            pltpu.VMEM((cells, phi_width), f32),
        ),
        in_specs=[anywhere] * 15,
        out_specs=(vm, vm),
        scratch_shapes=[
            buf(1, elements), buf(1, elements), buf(1, elements), buf(1, elements),
            ints(1, elements), ints(2, points), buf(2, points), buf(1, points), ints(1, points),
            ints(1, points), buf(9, cells, phi_width), pltpu.VMEM(basis.shape[1:], jnp.bfloat16),
            buf(*tiles.shape),
            buf(2 * comps * nr + 2, cols, width), buf(2, 2 * comps * nr + 2, cols, width),
            buf(2 * comps, cols, width), buf(2 * comps, cols, width),
            buf(comps, cols, width), buf(comps, cols, width),
            buf(n, 8, width), buf(n, comps, slot, width), buf(n // 2 + 1, 3 * cells, width),
            buf(az, 9, cells, phi_width),
            buf(az, cells, phi_width), buf(az, cells, phi_width),
            buf(2, az, layers, phi_width), buf(2, az, layers, phi_width),
            dma((2,)), dma((2,)), dma, dma, dma, dma, dma((n,)), dma((n,)),
            dma((az,)), dma((az,)), dma((az,)), dma((az,)),
            dma((n,)), dma((n,)), dma((n,)), dma((n,)),
            dma((az,)), dma((az,)), dma((2, az)), dma((2, az)), dma((15,)),
        ],
        compiler_params=pltpu.CompilerParams(
            collective_id=0, has_side_effects=True, vmem_limit_bytes=40 * 1024 * 1024
        ),
    )(
        *(
            pltpu.with_memory_space_constraint(x, pltpu.HBM)
            for x in (
                disp.reshape(comps * nr, cols, width), vel.reshape(comps * nr, cols, width),
                modulus, hoop, coupling, density, orders, element.T, local.T,
                scale.reshape(1, points), owner.T, cell.reshape(1, points),
                adjoint.reshape(9, cells, phi_width), jnp.asarray(basis), jnp.asarray(tiles),
            )
        )
    )
    return final, smoothed.reshape(layers, lats, phi_width)


def solution(mesh):
    field = P(None, None, "mer", "az")
    placed = (
        field, field, P(None, "mer"), P(None, "mer"), P(None, "mer"), P(None, "mer"),
        P(None, "mer"), P("mer", None), P("mer", None), P("mer"), P("mer", None), P("mer"), field,
    )
    return jax.shard_map(
        functools.partial(on_device, mesh.shape["mer"], mesh.shape["az"]),
        mesh=mesh,
        in_specs=placed,
        out_specs=(field, P(None, "mer", "az")),
        check_vma=False,
    )
```

```python
import functools
import math

import jax
import jax.numpy as jnp
import ml_dtypes
import numpy as np
from jax import lax
from jax.experimental import pallas as pl
from jax.experimental.pallas import tpu as pltpu
from jax.sharding import PartitionSpec as P

ORDERS = 256
STEPS = 3
step_scale = 0.015
smooth_rate = 0.125
MESH = pl.DeviceIdType.MESH


def gll_tables():
    nodes = np.array([-1.0, -math.sqrt(3.0 / 7.0), 0.0, math.sqrt(3.0 / 7.0), 1.0])
    weights = np.array([0.1, 49.0 / 90.0, 32.0 / 45.0, 49.0 / 90.0, 0.1])
    monomials = np.zeros((5, 5))
    for j in range(5):
        poly = np.array([1.0])
        for l in range(5):
            if l != j:
                poly = np.convolve(poly, np.array([1.0, -nodes[l]]) / (nodes[j] - nodes[l]))
        monomials[j] = poly[::-1]
    slopes = monomials[:, 1:] * np.arange(1, 5)
    derivative = np.array(
        [[sum(slopes[j, p] * nodes[i] ** p for p in range(4)) for j in range(5)] for i in range(5)]
    )
    stiffness = derivative.T @ np.diag(weights) @ derivative
    return weights, monomials, slopes, stiffness


def point_table(elements, cols, lanes):
    _, monomials, slopes, _ = gll_tables()
    both = np.concatenate([monomials, slopes], axis=1)
    table = np.zeros((1 + elements, 9, cols, lanes), np.float32)
    table[0, :, 0:5] = both.T[:, :, None]
    for e in range(elements):
        for c in range(cols):
            if 0 <= c - 4 * e <= 4:
                table[1 + e, :, c] = both[c - 4 * e][:, None]
    return table.reshape(-1, cols, lanes)


def column_table(elements, cols, lanes):
    weights, _, _, stiffness = gll_tables()
    table = np.zeros((elements, cols + 2, cols, lanes), np.float32)
    for e in range(elements):
        for c in range(cols):
            b = c - 4 * e
            if not 0 <= b <= 4:
                continue
            table[e, 0, c] = weights[b]
            for d in range(cols):
                other = (c - d) % cols - 4 * e
                if 0 <= other <= 4:
                    table[e, 1 + d, c] = stiffness[b, other]
            if cols - 4 * e == 4:
                table[e, cols + 1, c] = stiffness[b, 4]
    return table


def rim_table(cols, lanes):
    _, _, _, stiffness = gll_tables()
    table = np.zeros((cols, cols, lanes), np.float32)
    for d in range(cols):
        for a in range(5):
            other = (a - d) % cols
            if other <= 4:
                table[d, a] = stiffness[a, other]
    return table


def basis_tables(az_count, width, phi_width):
    coefs, phis = az_count * width, az_count * phi_width
    k, j = np.arange(coefs)[:, None], np.arange(phis)[None, :]
    angles = (k // 2) * j % (2 * ORDERS) * (2.0 * math.pi / (2 * ORDERS))
    basis = np.where(k % 2 == 0, np.cos(angles), np.sin(angles)) / math.sqrt(ORDERS)
    basis = basis.reshape(az_count, width, az_count, phi_width)
    turned = [
        np.concatenate([basis[q, :, (q + h) % az_count] for h in range(az_count)], axis=1)
        for q in range(az_count)
    ]
    basis = np.stack(turned).astype(np.float32)
    high = basis.astype(ml_dtypes.bfloat16)
    low = (basis - high.astype(np.float32)).astype(ml_dtypes.bfloat16)
    return np.concatenate([high, high, low], axis=1)


def halves(x):
    high = x.astype(jnp.bfloat16)
    return high, (x - high.astype(jnp.float32)).astype(jnp.bfloat16)


def dot(x, y):
    return jnp.dot(x, y, preferred_element_type=jnp.float32)


def left_parts(x):
    high, low = halves(x)
    return jnp.concatenate([high, low, high], axis=1)


def right_parts(x):
    high, low = halves(x)
    return jnp.concatenate([high, high, low], axis=0)


def kernel(
    n, az, disp_a, vel_a, modulus_a, hoop_a, coupling_a, density_a, orders_a, element_a, local_a,
    scale_a, owner_a, cell_a, adjoint_a, basis_a, tiles_a, out_u, out_k,
    modulus, hoop, coupling, density, orders, element, local, scale, owner, cell,
    adjoint, basis, tiles,
    halo_out, halo_in, edge_out, edge_in, half_out, half_in, meta, gathered, mix,
    adj_all, part_out, part_in, face_out, face_in,
    halo_s, halo_r, edge_s, edge_r, f_s, f_r, meta_s, meta_r, aa_s, aa_r, ab_s, ab_r, ga_s, ga_r, gb_s, gb_r,
    part_s, part_r, face_s, face_r, in_s,
):
    o, q = lax.axis_index("mer"), lax.axis_index("az")
    comps, nr, cols, width = out_u.shape
    fields = comps * nr
    elements = modulus.shape[1]
    points = owner.shape[1]
    slot = gathered.shape[2]
    nodes = nr * cols
    cells = adjoint.shape[1]
    depth = face_in.shape[2]
    lats = cells // depth
    weights, _, _, stiffness = gll_tables()
    has_left, has_right = o > 0, o < n - 1
    has_left_2, has_right_2 = o > 1, o < n - 2
    pairs = [
        (disp_a, halo_out.at[0:fields]), (vel_a, halo_out.at[fields : 2 * fields]), (modulus_a, modulus), (hoop_a, hoop), (coupling_a, coupling),
        (density_a, density), (orders_a, orders), (element_a, element), (local_a, local),
        (scale_a, scale), (owner_a, owner), (cell_a, cell), (tiles_a, tiles), (adjoint_a, adjoint),
        (basis_a.at[q], basis),
    ]
    fetches = [pltpu.make_async_copy(src, dst, in_s.at[i]) for i, (src, dst) in enumerate(pairs)]
    for fetch in fetches:
        fetch.start()

    halo_in[...] = jnp.zeros_like(halo_in)
    edge_in[...] = jnp.zeros_like(edge_in)
    half_in[...] = jnp.zeros_like(half_in)
    face_in[...] = jnp.zeros_like(face_in)
    gathered[:, :, nodes:, :] = jnp.zeros((n, comps, slot - nodes, width), jnp.float32)

    barrier = pltpu.get_barrier_semaphore()

    @pl.loop(1, n)
    def _(h):
        pl.semaphore_signal(barrier, inc=1, device_id=(lax.rem(o + h, n), q), device_id_type=MESH)

    for h in range(1, az):
        r = lax.rem(q + h, az)
        pl.semaphore_signal(barrier, inc=1, device_id=(o, r), device_id_type=MESH)

        @pl.when(has_left)
        def _():
            pl.semaphore_signal(barrier, inc=1, device_id=(o - 1, r), device_id_type=MESH)

        @pl.when(has_right)
        def _():
            pl.semaphore_signal(barrier, inc=1, device_id=(o + 1, r), device_id_type=MESH)

    for fetch in fetches[:-2]:
        fetch.wait()

    row = lax.broadcasted_iota(jnp.int32, (cols, width), 0)
    lane = lax.broadcasted_iota(jnp.int32, (1, width), 1)

    def field(ref, kind):
        at = lambda s, a: ref[kind * fields + s * nr + a]
        return [jnp.stack([at(s, a) for s in range(comps)]) for a in range(nr)]

    u, v = field(halo_out, 0), field(halo_out, 1)

    def first_column(values):
        total = jnp.zeros((comps, cols, width), jnp.float32)
        for a in range(nr):
            total = jnp.where((row == a)[None], values[a][:, 0:1, :], total)
        return total

    edge_out[0:comps] = first_column(u)
    edge_out[comps:] = first_column(v)
    one = lambda ref, e: ref[0:1, e : e + 1].astype(jnp.float32)
    known = jnp.zeros((2 * cols, width), jnp.float32)
    row_2 = lax.broadcasted_iota(jnp.int32, (2 * cols, width), 0)
    for i, ref in enumerate((modulus, hoop, coupling, density, orders)):
        for e in range(elements):
            known = jnp.where(row_2 == 5 * e + i, one(ref, e), known)
    halo_out[2 * fields] = known[0:cols]
    halo_out[2 * fields + 1] = known[cols:]
    halves_at = (fields + 1) // 2
    for k in range(halves_at):
        tile = halo_out[k]
        if k + halves_at < fields:
            tile = jnp.where(
                row >= cols // 2, tile, pltpu.roll(halo_out[k + halves_at], cols // 2, 0)
            )
        half_out[k] = tile
    half_out[halves_at] = known[0:cols]
    half_out[halves_at + 1] = known[cols:]
    spare = jnp.zeros((1, width - points), jnp.float32) if width > points else None

    def wide(line):
        return line if spare is None else jnp.concatenate([line, spare], axis=1)

    meta[o] = jnp.concatenate(
        [
            wide(local[0:1, :]),
            wide(local[1:2, :]),
            wide((element[1:2, :] % elements).astype(jnp.float32)),
            wide(owner[...].astype(jnp.float32)),
            wide(scale[...]),
            wide(cell[...].astype(jnp.float32)),
            jnp.zeros((2, width), jnp.float32),
        ],
        axis=0,
    )

    pl.semaphore_wait(
        barrier,
        n - 1 + (az - 1) * (1 + has_left.astype(jnp.int32) + has_right.astype(jnp.int32)),
    )

    def remote(src, dst, send, recv, device):
        return pltpu.make_async_remote_copy(
            src_ref=src, dst_ref=dst, send_sem=send, recv_sem=recv,
            device_id=device, device_id_type=MESH,
        )

    def to_left():
        return remote(halo_out, halo_in.at[1], halo_s.at[0], halo_r.at[0], (o - 1, q))

    def to_right():
        return remote(halo_out, halo_in.at[0], halo_s.at[1], halo_r.at[1], (o + 1, q))

    def to_right_2():
        return remote(half_out, half_in, f_s, f_r, (o + 2, q))

    def to_left_2():
        return remote(edge_out, edge_in, edge_s, edge_r, (o - 2, q))

    def meta_copy(h):
        return remote(meta.at[o], meta.at[o], meta_s.at[h], meta_r.at[h], (lax.rem(o + h, n), q))

    pl.loop(1, n)(lambda h: meta_copy(h).start())
    pl.when(has_left)(lambda: to_left().start())
    pl.when(has_right)(lambda: to_right().start())
    pl.when(has_left_2)(lambda: to_left_2().start())
    pl.when(has_right_2)(lambda: to_right_2().start())

    q_lo, q_hi, q_groups = lax.rem(q, 2), lax.div(q, 2), az // 2
    q_partner = q_hi * 2 + 1 - q_lo

    def adj_far(h):
        to = lax.rem(q_hi + h, q_groups) * 2 + q_lo
        return remote(adjoint, adj_all.at[q], aa_s.at[h], aa_r.at[h], (o, to))

    def adj_near(h):
        at = lax.rem(q_hi + q_groups - h, q_groups) * 2 + q_lo
        src = adjoint if h == 0 else adj_all.at[at]
        return remote(src, adj_all.at[at], ab_s.at[h], ab_r.at[h], (o, q_partner))

    fetches[-2].wait()
    for h in range(1, q_groups):
        adj_far(h).start()
    adj_near(0).start()

    order = (q * width + lane) // 2
    ratio = order.astype(jnp.float32) / ORDERS
    even = (lane % 2 == 0)
    last = elements - 1
    w_end = float(weights[4])
    points_at = 0
    cols_at = 9 * (1 + elements)
    rim_at = cols_at + elements * (cols + 2)
    cols_t = lambda e, which: tiles[cols_at + e * (cols + 2) + which]
    w_rim = jnp.zeros((cols, width), jnp.float32)
    for a in range(nr):
        w_rim = jnp.where(row == a, float(weights[a]), w_rim)

    def setup(ref, base, before, there):
        def value(i, e):
            at = 5 * e + i
            return ref[base + at // cols, at % cols : at % cols + 1, :]

        def blend(per_element, which):
            total = per_element[0] * cols_t(0, which)
            for e in range(1, elements):
                total = total + per_element[e] * cols_t(e, which)
            return total

        keep = [jnp.where(order.astype(jnp.float32) < value(4, e), 1.0, 0.0) for e in range(elements)]
        mod = [value(0, e) * keep[e] for e in range(elements)]
        hp = [value(1, e) * keep[e] * (ratio * ratio) for e in range(elements)]
        cp = [value(2, e) * keep[e] * ratio for e in range(elements)]
        c_radial, c_hoop, c_pair = blend(mod, 0), blend(hp, 0), blend(cp, 0)
        c_colat = [blend(mod, 1 + d) for d in range(cols)]
        c_rim = mod[last] * cols_t(last, cols + 1)
        r_radial = [mod[last] * w_end * tiles[rim_at + d] for d in range(cols)]
        r_radial[0] = r_radial[0] + w_rim * (
            mod[last] * float(stiffness[4, 4]) + hp[last] * w_end
        )
        r_pair = w_rim * (cp[last] * w_end)
        mass = blend([value(3, e) for e in range(elements)], 0)
        if before is not None:
            at = 5 * last + 3
            ref_2, base_2 = before
            shared = ref_2[base_2 + at // cols, at % cols : at % cols + 1, :]
            mass = mass + jnp.where(row == 0, w_end * shared, 0.0)
        inverse = [step_scale / (float(weights[a]) * mass) for a in range(nr)]
        if there is not None:
            inverse = [jnp.where(there, x, 0.0) for x in inverse]
        return (c_radial, c_hoop, c_pair, c_colat, c_rim, r_radial, r_pair), inverse

    def swap(x):
        axis = x.ndim - 1
        return jnp.where(even, pltpu.roll(x, width - 1, axis), -pltpu.roll(x, 1, axis))

    def pair(x, factor):
        return jnp.stack(
            [factor * swap(x[2]), jnp.zeros((cols, width), jnp.float32), -factor * swap(x[0])]
        )

    def main_force(u, rim, coefs):
        c_radial, c_hoop, c_pair, c_colat, c_rim, _, _ = coefs
        forces = []
        for a in range(nr):
            w_a = float(weights[a])
            colat = c_rim * rim[:, a : a + 1, :] + c_colat[0] * u[a]
            for d in range(1, cols):
                colat = colat + c_colat[d] * pltpu.roll(u[a], d, 1)
            radial = float(stiffness[a, 0]) * u[0]
            for i in range(1, nr):
                radial = radial + float(stiffness[a, i]) * u[i]
            force = pair(u[a], w_a * c_pair) - (
                c_radial * radial + w_a * (colat + c_hoop * u[a])
            )
            forces.append(force)
        return forces

    def end_force(u, rim, coefs):
        c_rim, r_radial, r_pair = coefs[4:]
        force = jnp.zeros((comps, cols, width), jnp.float32)
        for a in range(nr):
            ending = jnp.sum(c_rim * u[a], axis=1, keepdims=True)
            force = jnp.where((row == a)[None], -float(weights[a]) * ending, force)
        force = force + pair(rim, r_pair)
        for d in range(cols):
            force = force - r_radial[d] * (pltpu.roll(rim, d, 1) if d else rim)
        return force

    def with_edge(forces, edge):
        return [
            forces[a] + jnp.where((row == 0)[None], edge[:, a : a + 1, :], 0.0) for a in range(nr)
        ]

    def advance(u, before, forces, inverse):
        return [2.0 * u[a] - before[a] + inverse[a] * forces[a] for a in range(nr)]

    wanted = lax.broadcasted_iota(jnp.int32, (cells, width), 0).astype(jnp.float32)
    upper = lane >= slot
    blank = jnp.zeros((slot - nodes, width), jnp.float32)
    _, monomials, slopes, _ = gll_tables()

    def horner(x, coefs):
        total = coefs[-1]
        for coef in coefs[-2::-1]:
            total = total * x + coef
        return total

    def tile_horner(x, at, count):
        return horner(x, [tiles[points_at + at + p] for p in range(count)])

    def block_mix(i):
        line = lambda k: meta[i, k : k + 1, :]
        xi, eta, spot, factor = line(0), line(1), line(2), line(4)
        l_xi, s_xi = tile_horner(xi, 0, 5), tile_horner(xi, 5, 4)
        l_eta, s_eta = tile_horner(eta, 9, 5), tile_horner(eta, 14, 4)
        for e in range(1, elements):
            here = spot == float(e)
            l_eta = jnp.where(here, tile_horner(eta, 9 + 9 * e, 5), l_eta)
            s_eta = jnp.where(here, tile_horner(eta, 14 + 9 * e, 4), s_eta)
        at_end = spot == float(elements - 1)
        l_end = jnp.where(at_end, horner(eta, [float(x) for x in monomials[4]]), 0.0)
        s_end = jnp.where(at_end, horner(eta, [float(x) for x in slopes[4]]), 0.0)
        parts = []
        for x, y, y_end in (
            (s_xi, l_eta, l_end), (l_xi, s_eta, s_end), (factor * l_xi, l_eta, l_end)
        ):
            parts += [x[a : a + 1, :] * y for a in range(nr)] + [blank]
            end = x * y_end
            parts += [jnp.where(row == 0, end[a : a + 1, :], 0.0) for a in range(nr)] + [blank]
        high, low = halves(jnp.concatenate(parts, axis=0))
        chosen = (line(3) == o.astype(jnp.float32)) & (line(5) == wanted)
        chosen = chosen & (lane < points)
        chosen = jnp.where(chosen, 1.0, 0.0).astype(jnp.bfloat16)
        taken = lax.dot_general(
            jnp.concatenate([chosen, chosen], axis=1),
            jnp.concatenate([high, low], axis=1),
            (((1,), (1,)), ((), ())),
            preferred_element_type=jnp.float32,
        )
        return jnp.concatenate([taken[:, t * width : (t + 1) * width] for t in range(3)], axis=0)

    def mix_blocks(start, stop):
        @pl.loop(start, stop)
        def _(j):
            first, second = block_mix(2 * j), pltpu.roll(block_mix(2 * j + 1), slot, 1)
            mix[j] = mix[j] + first + jnp.where(upper, second, 0.0)
            mix[j + 1] = mix[j + 1] + jnp.where(upper, 0.0, second)

    pl.loop(1, n)(lambda h: meta_copy(h).wait_recv())
    mix[...] = jnp.zeros_like(mix)
    mix_blocks(0, n // 2)

    pl.when(has_right)(lambda: to_left().wait_recv())
    pl.when(has_left)(lambda: to_right().wait_recv())
    pl.when(has_right_2)(lambda: to_left_2().wait_recv())
    pl.when(has_left_2)(lambda: to_right_2().wait_recv())
    left, right = halo_in.at[0], halo_in.at[1]
    known_at = 2 * fields
    coefs_ll, _ = setup(half_in, halves_at, None, has_left_2)
    coefs_l, inverse_l = setup(left, known_at, (half_in, halves_at), has_left)
    coefs_m, inverse_m = setup(halo_out, known_at, (left, known_at), None)
    coefs_r, inverse_r = setup(right, known_at, (halo_out, known_at), has_right)
    half_tiles = [half_in[k] for k in range(halves_at)]
    half_tiles += [pltpu.roll(half_in[k], cols // 2, 0) for k in range(fields - halves_at)]
    u_ll = [jnp.stack([half_tiles[s * nr + a] for s in range(comps)]) for a in range(nr)]
    u_l, u_r = field(left, 0), field(right, 0)
    before_l = [x - y for x, y in zip(u_l, field(left, 1))]
    before = [x - y for x, y in zip(u, v)]
    before_r = [x - y for x, y in zip(u_r, field(right, 1))]
    far_rim = edge_in[0:comps]

    rim_l, rim = first_column(u), first_column(u_r)
    force_l = with_edge(
        main_force(u_l, rim_l, coefs_l), end_force(u_ll, first_column(u_l), coefs_ll)
    )
    force_m = with_edge(main_force(u, rim, coefs_m), end_force(u_l, rim_l, coefs_l))
    force_r = with_edge(main_force(u_r, far_rim, coefs_r), end_force(u, rim, coefs_m))
    before_l, u_l = u_l, advance(u_l, before_l, force_l, inverse_l)
    before, u = u, advance(u, before, force_m, inverse_m)
    before_r, u_r = u_r, advance(u_r, before_r, force_r, inverse_r)

    rim_l, rim = first_column(u), first_column(u_r)
    force_m = with_edge(main_force(u, rim, coefs_m), end_force(u_l, rim_l, coefs_l))
    force_r = with_edge(main_force(u_r, far_rim, coefs_r), end_force(u, rim, coefs_m))
    before, u = u, advance(u, before, force_m, inverse_m)
    u_l = advance(u_l, before_l, main_force(u_l, rim_l, coefs_l), inverse_l)
    u_r = advance(u_r, before_r, force_r, inverse_r)

    rim_l, rim = first_column(u), first_column(u_r)
    force_m = with_edge(main_force(u, rim, coefs_m), end_force(u_l, rim_l, coefs_l))
    u = advance(u, before, force_m, inverse_m)

    for a in range(nr):
        gathered[o, :, a * cols : (a + 1) * cols, :] = u[a]
    lo, hi, groups = lax.rem(o, 2), lax.div(o, 2), n // 2
    partner = hi * 2 + 1 - lo

    def far(h):
        block = gathered.at[o, :, 0:nodes, :]
        to = lax.rem(hi + h, groups) * 2 + lo
        return remote(block, block, ga_s.at[h], ga_r.at[h], (to, q))

    def near(h):
        block = gathered.at[lax.rem(hi + groups - h, groups) * 2 + lo, :, 0:nodes, :]
        return remote(block, block, gb_s.at[h], gb_r.at[h], (partner, q))

    pl.loop(1, groups)(lambda h: far(h).start())
    near(0).start()
    for h in range(1, q_groups):
        adj_far(h).wait_recv()
        adj_near(h).start()
    for a in range(nr):
        out_u[:, a] = u[a]

    def add_group(h, total):
        near(h).wait_recv()
        j = lax.rem(hi + groups - h, groups)
        block = [
            jnp.concatenate([gathered[2 * j, s], gathered[2 * j + 1, s]], axis=0)
            for s in range(comps)
        ]
        return total + dot(left_parts(mix[j]), right_parts(jnp.concatenate(block, axis=1)))

    def next_group(h, total):
        far(h).wait_recv()
        near(h).start()
        return add_group(h - 1, total)

    coefs = lax.fori_loop(
        1, groups, next_group, jnp.zeros((3 * cells, comps * width), jnp.float32)
    )
    coefs = add_group(groups - 1, coefs)
    fetches[-1].wait()
    for h in range(q_groups):
        adj_near(h).wait_recv()
    coefs = [coefs[:, s * width : (s + 1) * width] for s in range(comps)]
    rows = []
    for s in range(comps):
        rows.append(coefs[s][0 : 2 * cells])
        rows.append(swap(coefs[s][2 * cells :]) * ratio)
    samples = dot(left_parts(jnp.concatenate(rows, axis=0)), basis[...])
    raw = []
    for h in range(az):
        total = jnp.zeros((cells, width), jnp.float32)
        for g in range(3 * comps):
            values = adjoint[g] if h == 0 else adj_all[lax.rem(q + h, az), g]
            at = samples[g * cells : (g + 1) * cells, h * width : (h + 1) * width]
            total = total + at * values
        raw.append(total)
    raw = jnp.concatenate(raw, axis=1)
    whole = az * width
    tile_lat = lax.broadcasted_iota(jnp.int32, (depth, width), 0) % lats
    for h in range(az):
        low_face = jnp.zeros((depth, width), jnp.float32)
        high_face = jnp.zeros((depth, width), jnp.float32)
        for i in range(cells // depth):
            tile = raw[i * depth : (i + 1) * depth, h * width : (h + 1) * width]
            first = pltpu.roll(jnp.where(tile_lat == 0, tile, 0.0), i, 0) if i else (
                jnp.where(tile_lat == 0, tile, 0.0)
            )
            low_face = low_face + first
            turn = (i + depth - (lats - 1)) % depth
            final_row = jnp.where(tile_lat == lats - 1, tile, 0.0)
            high_face = high_face + (pltpu.roll(final_row, turn, 0) if turn else final_row)
        face_out[0, h] = low_face
        face_out[1, h] = high_face

    def face_left(h):
        return remote(
            face_out.at[0, h], face_in.at[1, h], face_s.at[0, h], face_r.at[0, h],
            (o - 1, lax.rem(q + h, az)),
        )

    def face_right(h):
        return remote(
            face_out.at[1, h], face_in.at[0, h], face_s.at[1, h], face_r.at[1, h],
            (o + 1, lax.rem(q + h, az)),
        )

    for h in range(az):
        pl.when(has_left)(lambda: face_left(h).start())
        pl.when(has_right)(lambda: face_right(h).start())
    level = lax.broadcasted_iota(jnp.int32, (cells, whole), 0)
    lat = level % lats
    around = pltpu.roll(raw, 1, 1) + pltpu.roll(raw, whole - 1, 1)
    around = around + jnp.where(lat > 0, pltpu.roll(raw, 1, 0), 0.0)
    around = around + jnp.where(lat < lats - 1, pltpu.roll(raw, cells - 1, 0), 0.0)
    around = around + jnp.where(level >= lats, pltpu.roll(raw, lats, 0), 0.0)
    around = around + jnp.where(level < cells - lats, pltpu.roll(raw, cells - lats, 0), 0.0)
    smooth = (1.0 - 6.0 * smooth_rate) * raw + smooth_rate * around

    def part_copy(h):
        return remote(
            part_out.at[h], part_in.at[h], part_s.at[h], part_r.at[h], (o, lax.rem(q + h, az))
        )

    for h in range(1, az):
        part_out[h] = smooth[:, h * width : (h + 1) * width]
        part_copy(h).start()
    result = smooth[:, 0:width]
    for h in range(1, az):
        part_copy(h).wait_recv()
        result = result + part_in[h]
    for h in range(az):
        pl.when(has_right)(lambda: face_left(h).wait_recv())
        pl.when(has_left)(lambda: face_right(h).wait_recv())
    below, above = face_in[0, 0], face_in[1, 0]
    for h in range(1, az):
        below, above = below + face_in[0, h], above + face_in[1, h]
    for i in range(cells // depth):
        turn = (lats - 1 - i) % depth
        first = pltpu.roll(below, (depth - i) % depth, 0) if i else below
        final_row = pltpu.roll(above, turn, 0) if turn else above
        extra = jnp.where(tile_lat == 0, first, 0.0) + jnp.where(
            tile_lat == lats - 1, final_row, 0.0
        )
        at = slice(i * depth, (i + 1) * depth)
        out_k[at] = result[at] + smooth_rate * extra

    pl.when(has_left)(lambda: to_left().wait_send())
    pl.when(has_right)(lambda: to_right().wait_send())
    pl.loop(1, n)(lambda h: meta_copy(h).wait_send())
    pl.when(has_left_2)(lambda: to_left_2().wait_send())
    pl.when(has_right_2)(lambda: to_right_2().wait_send())
    for h in range(q_groups):
        adj_near(h).wait_send()
        if h:
            adj_far(h).wait_send()
    for h in range(1, az):
        part_copy(h).wait_send()
    for h in range(az):
        pl.when(has_left)(lambda: face_left(h).wait_send())
        pl.when(has_right)(lambda: face_right(h).wait_send())
    pl.loop(1, groups)(lambda h: far(h).wait_send())
    pl.loop(0, groups)(lambda h: near(h).wait_send())


def on_device(
    n, az, disp, vel, modulus, hoop, coupling, density, orders, element, local, scale, owner, cell,
    adjoint,
):
    comps, nr, cols, width = disp.shape
    elements, points = modulus.shape[1], owner.shape[0]
    layers, lats, phi_width = adjoint.shape[1:]
    cells = layers * lats
    assert STEPS == 3 and elements == 2
    assert nr == 5 and cols == 4 * elements and layers == 8 and layers % lats == 0
    assert points <= width and width == phi_width
    tiles = np.concatenate(
        [
            point_table(elements, cols, width),
            column_table(elements, cols, width).reshape(-1, cols, width),
            rim_table(cols, width),
        ]
    )
    basis = basis_tables(az, width, phi_width)
    vm = pl.BlockSpec(memory_space=pltpu.VMEM)
    anywhere = pl.BlockSpec(memory_space=pltpu.HBM)
    slot = width // 2
    f32, dma = jnp.float32, pltpu.SemaphoreType.DMA
    buf = lambda *shape: pltpu.VMEM(shape, f32)
    ints = lambda *shape: pltpu.VMEM(shape, jnp.int32)
    final, smoothed = pl.pallas_call(
        functools.partial(kernel, n, az),
        out_shape=(
            pltpu.VMEM(disp.shape, f32),
            pltpu.VMEM((cells, phi_width), f32),
        ),
        in_specs=[anywhere] * 15,
        out_specs=(vm, vm),
        scratch_shapes=[
            buf(1, elements), buf(1, elements), buf(1, elements), buf(1, elements),
            ints(1, elements), ints(2, points), buf(2, points), buf(1, points), ints(1, points),
            ints(1, points), buf(9, cells, phi_width), pltpu.VMEM(basis.shape[1:], jnp.bfloat16),
            buf(*tiles.shape),
            buf(2 * comps * nr + 2, cols, width), buf(2, 2 * comps * nr + 2, cols, width),
            buf(2 * comps, cols, width), buf(2 * comps, cols, width),
            buf((comps * nr + 1) // 2 + 2, cols, width), buf((comps * nr + 1) // 2 + 2, cols, width),
            buf(n, 8, width), buf(n, comps, slot, width), buf(n // 2 + 1, 3 * cells, width),
            buf(az, 9, cells, phi_width),
            buf(az, cells, phi_width), buf(az, cells, phi_width),
            buf(2, az, layers, phi_width), buf(2, az, layers, phi_width),
            dma((2,)), dma((2,)), dma, dma, dma, dma, dma((n,)), dma((n,)),
            dma((az,)), dma((az,)), dma((az,)), dma((az,)),
            dma((n,)), dma((n,)), dma((n,)), dma((n,)),
            dma((az,)), dma((az,)), dma((2, az)), dma((2, az)), dma((15,)),
        ],
        compiler_params=pltpu.CompilerParams(
            collective_id=0, has_side_effects=True, vmem_limit_bytes=40 * 1024 * 1024
        ),
    )(
        *(
            pltpu.with_memory_space_constraint(x, pltpu.HBM)
            for x in (
                disp.reshape(comps * nr, cols, width), vel.reshape(comps * nr, cols, width),
                modulus, hoop, coupling, density, orders, element.T, local.T,
                scale.reshape(1, points), owner.T, cell.reshape(1, points),
                adjoint.reshape(9, cells, phi_width), jnp.asarray(basis), jnp.asarray(tiles),
            )
        )
    )
    return final, smoothed.reshape(layers, lats, phi_width)


def solution(mesh):
    field = P(None, None, "mer", "az")
    placed = (
        field, field, P(None, "mer"), P(None, "mer"), P(None, "mer"), P(None, "mer"),
        P(None, "mer"), P("mer", None), P("mer", None), P("mer"), P("mer", None), P("mer"), field,
    )
    return jax.shard_map(
        functools.partial(on_device, mesh.shape["mer"], mesh.shape["az"]),
        mesh=mesh,
        in_specs=placed,
        out_specs=(field, P(None, "mer", "az")),
        check_vma=False,
    )
```
